128 devices in a mesh: occ: 16 (over x, y), vir: 8 (over z, core).
Axes of the slice: x: 4, y: 4, z: 4, core: 2. Of those that a mesh axis runs over, the one named last changes fastest.
Arguments:
- t_tiles: bfloat16 [16384, 9216], P(('occ', 'vir')), may hold values from -6 to 6
- t_index: int32 [16384, 3], P(('occ', 'vir')), may hold values from 0 to 255, as said below
- cycle_map: int32 [256], replicated, may hold values from 0 to 15, as said below
- ladder_slots: int32 [3072, 3], P('occ'), may hold values from 0 to 47, as said below
- cycle_slots: int32 [3072, 3], P('occ'), may hold values from 0 to 47, as said below
- x_ints: bfloat16 [4608, 4608], P('occ', 'vir'), may hold values from -0.375 to 0.375
- y_ints: bfloat16 [4608, 4608], P('vir', 'occ'), may hold values from -0.375 to 0.375
Outputs:
- ladder_resid: float32 [3072, 9216], P(('occ', 'vir'))
- cycle_resid: float32 [3072, 9216], P(('occ', 'vir'))
The draws below stay inside these ranges and needn't reach their ends.
Inputs may be any that keep to these rules, and one draw needn't show every extreme that they name: `t_index`: tile k on device (o, v) has p_k in o * 16 to o * 16 + 15 and c_k in v * 6 to v * 6 + 5; no two tiles share (p, c, d). Each pair has a domain of 8 virtual tiles, and its tiles are exactly those with c and d both in its domain. Taking a tile's cycle owner as the device (cycle_map[p_k], d_k // 6), every device holds at most 4 tiles for one cycle owner, and exactly 4 for some owner. For each group g and local index s exactly one o has cycle_map[o * 16 + s] = g, so the 16 pairs of one occ group go to 16 different groups. `ladder_slots`: the first entry of a row is below 16; a and b lie in the domain of the row's pair. `cycle_slots`: the first entry of a row is below 16; a and b lie in the domain of the row's pair.
All inputs are finite; a program needn't handle non-finite values.
Results may differ from the reference program's by a relative error of at most 0.012.
Values may be sent and summed in bfloat16 or wider, within the bound.
A program may use at most 128 MiB of HBM per device.

```python
import math
import jax
import jax.numpy as jnp
from jax import lax

TILE = 96
NV = 48
DOM = 8
NR = 192
VT = 6
PAIRS = 16
NPAIR = 256
NT = 128
TILES = 16384
SLOTS = 3072
N_OCC = 16
N_VIR = 8
DEVICES = 128


def owner_groups(key):
    key = jax.random.fold_in(key, 11)
    shuffled = jax.random.permutation(key, N_OCC).astype(jnp.int32)
    groups = jnp.arange(N_OCC, dtype=jnp.int32)[:, None]
    local_ids = jnp.arange(PAIRS, dtype=jnp.int32)[None, :]
    return shuffled[(groups + local_ids) % N_OCC].reshape(NPAIR).astype(jnp.int32)


def pair_domains(key):
    key = jax.random.fold_in(key, 12)
    key_start, key_first, key_step = jax.random.split(key, 3)
    spans = DOM // 2
    starts = jax.random.randint(key_start, (N_OCC,), 0, N_VIR).astype(jnp.int32)
    firsts = jax.random.randint(key_first, (NPAIR, spans), 0, VT).astype(jnp.int32)
    offsets = jax.random.randint(key_step, (NPAIR, spans), 1, VT).astype(jnp.int32)
    seconds = (firsts + offsets) % VT
    pair_ids = jnp.arange(NPAIR, dtype=jnp.int32)
    group_ids = pair_ids // PAIRS
    local_ids = pair_ids % PAIRS
    span_ids = jnp.arange(spans, dtype=jnp.int32)
    cover = (local_ids[:, None] + starts[group_ids][:, None] + span_ids[None, :]) % N_VIR
    domain = jnp.stack([cover * VT + firsts, cover * VT + seconds], axis=2).reshape(NPAIR, DOM)
    return (starts, domain.astype(jnp.int32))


def draw_cycle_map(key, part):
    return owner_groups(key)


def draw_t_index(key, part):
    starts, domain = pair_domains(key)
    key = jax.random.fold_in(key, 4)
    spans = DOM // 2
    repeats = PAIRS // N_VIR
    device_ids = jnp.arange(DEVICES, dtype=jnp.int32)
    occ_ids = device_ids // N_VIR
    vir_ids = device_ids % N_VIR
    span_ids = jnp.arange(spans, dtype=jnp.int32)
    repeat_ids = jnp.arange(repeats, dtype=jnp.int32)
    first_ids = jnp.arange(2, dtype=jnp.int32)
    local_base = (vir_ids[:, None] - starts[occ_ids][:, None] - span_ids[None, :]) % N_VIR
    local_ids = local_base[:, :, None] + repeat_ids[None, None, :] * N_VIR
    pair_ids = occ_ids[:, None, None] * PAIRS + local_ids
    column_ids = 2 * span_ids[None, :, None, None] + first_ids[None, None, None, :]
    first_tiles = domain[pair_ids[..., None], column_ids]
    second_tiles = domain[pair_ids]
    full_shape = (DEVICES, spans, repeats, 2, DOM)
    pairs_full = jnp.broadcast_to(pair_ids[..., None, None], full_shape)
    first_full = jnp.broadcast_to(first_tiles[..., None], full_shape)
    second_full = jnp.broadcast_to(second_tiles[:, :, :, None, :], full_shape)
    labels = jnp.stack([pairs_full, first_full, second_full], axis=-1).reshape(DEVICES, NT, 3)
    device_keys = jax.random.split(key, DEVICES)
    orders = jax.vmap(lambda one_key: jax.random.permutation(one_key, NT))(device_keys).astype(jnp.int32)
    shuffled = jnp.take_along_axis(labels, orders[:, :, None], axis=1)
    return shuffled.reshape(TILES, 3).astype(jnp.int32)


def slot_entries(key, domain, pairs):
    key_first, key_second = jax.random.split(key, 2)
    first_pick = jax.random.randint(key_first, (SLOTS,), 0, DOM).astype(jnp.int32)
    second_pick = jax.random.randint(key_second, (SLOTS,), 0, DOM).astype(jnp.int32)
    return (domain[pairs, first_pick], domain[pairs, second_pick])


def draw_ladder_slots(key, part):
    starts, domain = pair_domains(key)
    key = jax.random.fold_in(key, 2)
    key_pair, key_rest = jax.random.split(key, 2)
    local_ids = jax.random.randint(key_pair, (SLOTS,), 0, PAIRS).astype(jnp.int32)
    groups = jnp.arange(SLOTS, dtype=jnp.int32) // NR
    pairs = groups * PAIRS + local_ids
    first_tiles, second_tiles = slot_entries(key_rest, domain, pairs)
    return jnp.stack([local_ids, first_tiles, second_tiles], axis=1).astype(jnp.int32)


def draw_cycle_slots(key, part):
    cycle_map = owner_groups(key)
    starts, domain = pair_domains(key)
    key = jax.random.fold_in(key, 3)
    key_pair, key_rest = jax.random.split(key, 2)
    local_ids = jax.random.randint(key_pair, (SLOTS,), 0, PAIRS).astype(jnp.int32)
    groups = jnp.arange(SLOTS, dtype=jnp.int32) // NR
    owner_table = cycle_map.reshape(N_OCC, PAIRS)
    group_range = jnp.arange(N_OCC, dtype=jnp.int32)
    anchors = jnp.sum(jnp.where(owner_table[:, local_ids] == groups[None, :], group_range[:, None], 0), axis=0)
    pairs = anchors * PAIRS + local_ids
    first_tiles, second_tiles = slot_entries(key_rest, domain, pairs)
    return jnp.stack([local_ids, first_tiles, second_tiles], axis=1).astype(jnp.int32)


def block_scale(own_key, extent, shards, smallest, top_value):
    level = 1.0
    for position, parts in shards:
        steps = jax.random.uniform(jax.random.fold_in(jax.random.fold_in(own_key, 6), position), (parts,), jnp.float32, smallest / len(shards), top_value / len(shards))
        level = level * jnp.repeat(jnp.exp(steps), extent[position] // parts).reshape((-1,) + (1,) * (len(extent) - 1 - position))
    return level


def scatter_about(rng, extent, width, limit, shards=(), kind=jnp.bfloat16):
    result = width * jax.random.normal(rng, extent, jnp.float32)
    if shards:
        result = result * block_scale(rng, extent, shards, -0.22, 0.18)
    return jnp.clip(result, -limit, limit).astype(kind)


def setup_inputs(seed: int = 0) -> dict:
    seeds = jax.random.split(jax.random.key(seed), 8)
    t_tiles = scatter_about(seeds[0], (TILES, TILE * TILE), 1.0, 6.0, ((0, 128),))
    t_index = draw_t_index(jax.random.fold_in(seeds[7], 71), 0)
    cycle_map = draw_cycle_map(jax.random.fold_in(seeds[7], 71), 0)
    ladder_slots = draw_ladder_slots(jax.random.fold_in(seeds[7], 71), 0)
    cycle_slots = draw_cycle_slots(jax.random.fold_in(seeds[7], 71), 0)
    x_ints = scatter_about(seeds[5], (NV * TILE, NV * TILE), (3 * TILE) ** -0.5, 0.375, ((0, 16), (1, 8)))
    y_ints = scatter_about(seeds[6], (NV * TILE, NV * TILE), (3 * TILE) ** -0.5, 0.375, ((0, 8), (1, 16)))
    return {"t_tiles": t_tiles, "t_index": t_index, "cycle_map": cycle_map, "ladder_slots": ladder_slots, "cycle_slots": cycle_slots, "x_ints": x_ints, "y_ints": y_ints}


def fetch_tiles(t_tiles, sorted_keys, ordering, queries):
    located = jnp.clip(jnp.searchsorted(sorted_keys, queries), 0, sorted_keys.shape[0] - 1).astype(jnp.int32)
    present = sorted_keys[located] == queries
    chosen = t_tiles[ordering[located]].astype(jnp.float32)
    return jnp.where(present[..., None], chosen, jnp.zeros((), jnp.float32))


def round_sum(partials):
    rounded = lax.optimization_barrier(partials.astype(jnp.bfloat16))
    return jnp.sum(rounded.astype(jnp.float32), axis=1)


def reference(t_tiles, t_index, cycle_map, ladder_slots, cycle_slots, x_ints, y_ints):
    tile_keys = (t_index[:, 0] * NV + t_index[:, 1]) * NV + t_index[:, 2]
    ordering = jnp.argsort(tile_keys).astype(jnp.int32)
    sorted_keys = tile_keys[ordering]
    tile_range = jnp.arange(NV, dtype=jnp.int32)
    x_blocks = x_ints.reshape(NV, TILE, N_VIR, VT, TILE)
    y_blocks = y_ints.reshape(N_VIR, VT, TILE, NV, TILE)
    owner_table = cycle_map.reshape(N_OCC, PAIRS)
    group_range = jnp.arange(N_OCC, dtype=jnp.int32)
    slot_groups = jnp.arange(SLOTS, dtype=jnp.int32) // NR
    batch = math.gcd(SLOTS, 32)

    def ladder_block(slot_item):
        slot_rows, groups = slot_item
        pairs = groups * PAIRS + slot_rows[:, 0]
        queries = (pairs[:, None] * NV + tile_range[None, :]) * NV + slot_rows[:, 2][:, None]
        picked = fetch_tiles(t_tiles, sorted_keys, ordering, queries).reshape(batch, N_VIR, VT, TILE, TILE)
        rows = x_blocks[slot_rows[:, 1]].astype(jnp.float32)
        partials = jnp.einsum("bxvcy,bvcyz->bvxz", rows, picked)
        return round_sum(partials).reshape(batch, TILE * TILE)

    def cycle_block(slot_item):
        slot_rows, groups = slot_item
        owners = jnp.sum(jnp.where(owner_table[:, slot_rows[:, 0]] == groups[None, :], group_range[:, None], 0), axis=0)
        pairs = owners * PAIRS + slot_rows[:, 0]
        queries = (pairs[:, None] * NV + slot_rows[:, 1][:, None]) * NV + tile_range[None, :]
        picked = fetch_tiles(t_tiles, sorted_keys, ordering, queries).reshape(batch, N_VIR, VT, TILE, TILE)
        columns = jnp.take(y_blocks, slot_rows[:, 2], axis=3).astype(jnp.float32)
        partials = jnp.einsum("bvcxy,vcybz->bvxz", picked, columns)
        return round_sum(partials).reshape(batch, TILE * TILE)

    groups_split = slot_groups.reshape(-1, batch)
    ladder_resid = lax.map(ladder_block, (ladder_slots.reshape(-1, batch, 3), groups_split)).reshape(SLOTS, TILE * TILE)
    cycle_resid = lax.map(cycle_block, (cycle_slots.reshape(-1, batch, 3), groups_split)).reshape(SLOTS, TILE * TILE)
    return ladder_resid, cycle_resid
```

```python
import functools

import jax
import jax.numpy as jnp
from jax import lax
from jax.experimental import pallas as pl
from jax.experimental.pallas import tpu as pltpu
from jax.sharding import PartitionSpec as P

TILE = 96
NV = 48
AREA = TILE * TILE
OCC = 16
VIR = 8
VT = 6
PAIRS = 16
VCAP = 32
BLOCKS = 288
ROWS = 192


def rows_kernel(swap, index_ref, table_ref, tiles_ref, out_ref, blocks):
    def unpack(row, carry):
        strip = table_ref[pl.ds(pl.multiple_of(row * TILE, TILE), TILE), :]
        for c in range(6):
            blocks[row * 6 + c] = strip[:, c * TILE : (c + 1) * TILE]
        return carry

    lax.fori_loop(0, NV, unpack, 0)
    blocks[BLOCKS] = jnp.zeros((TILE, TILE), blocks.dtype)

    def octet(q, carry):
        for j in range(8):
            row = q * 8 + j
            total = None
            for half in range(2):
                block = blocks[index_ref[half * ROWS + row]]
                tile = tiles_ref[index_ref[(2 + half) * ROWS + row]]
                left, right = (tile, block) if swap else (block, tile)
                part = jnp.dot(left, right, preferred_element_type=jnp.float32)
                total = part if total is None else total + part
            out_ref[q, :, j * TILE : (j + 1) * TILE] = total.astype(out_ref.dtype)
        return carry

    lax.fori_loop(0, ROWS // 8, octet, 0)


def rows_call(swap, index, table, tiles, name):
    return pl.pallas_call(
        functools.partial(rows_kernel, swap),
        out_shape=jax.ShapeDtypeStruct((ROWS // 8, TILE, 8 * TILE), jnp.bfloat16),
        in_specs=[
            pl.BlockSpec(memory_space=pltpu.SMEM),
            pl.BlockSpec(memory_space=pltpu.VMEM),
            pl.BlockSpec(memory_space=pltpu.VMEM),
        ],
        out_specs=pl.BlockSpec(memory_space=pltpu.VMEM),
        scratch_shapes=[pltpu.VMEM((BLOCKS + 1, TILE, TILE), jnp.bfloat16)],
        compiler_params=pltpu.CompilerParams(vmem_limit_bytes=48 * 1024 * 1024),
        cost_estimate=pl.CostEstimate(flops=2 * 2 * ROWS * TILE**3, bytes_accessed=14_000_000, transcendentals=0),
        name=name,
    )(index.reshape(-1), table, tiles)


def lookup(ids, table):
    flat = table.reshape(-1)
    hits = ids[..., None] == jnp.arange(flat.shape[0], dtype=jnp.int32)
    return jnp.sum(jnp.where(hits, flat, 0), axis=-1)


def before(counts, axis):
    return jnp.cumsum(counts, axis=axis) - counts


def on_device(t_tiles, t_index, cycle_map, ladder_slots, cycle_slots, x_ints, y_ints):
    occ = lax.axis_index("occ")
    vir = lax.axis_index("vir")
    i32 = jnp.int32
    local = t_index[:, 0] - occ * PAIRS
    first = t_index[:, 1] - vir * VT
    second = t_index[:, 2]

    marks = jnp.arange(PAIRS * VT, dtype=i32)[None, :] == (local * VT + first)[:, None]
    held = jnp.max(marks.astype(i32), axis=0)
    gathered = lax.all_gather(held, ("occ", "vir"), axis=0, tiled=False)
    domain = gathered.reshape(OCC, VIR, PAIRS, VT).transpose(0, 2, 1, 3)
    x_rows = lax.all_gather(x_ints, "occ", axis=0, tiled=True)
    y_pack = (
        y_ints.reshape(3, 2, TILE, 3, TILE).transpose(0, 2, 1, 3, 4).reshape(3 * TILE, 6 * TILE)
    )
    y_rows = lax.all_gather(y_pack, "occ", axis=0, tiled=True)

    def tables(dom):
        counts = jnp.sum(dom, axis=-1)
        rank_in = before(dom, 2)
        rank_all = rank_in + before(counts, 1)[..., None]
        return counts, rank_in, rank_all

    mine = lax.dynamic_index_in_dim(domain, occ, 0, keepdims=False)
    counts, rank_in, rank_all = tables(mine)
    products = counts[:, :, None] * counts[:, None, :]
    starts = before(products, 0)

    own_counts = lax.dynamic_index_in_dim(counts, vir, 1, keepdims=False)
    own_starts = lax.dynamic_index_in_dim(starts, vir, 1, keepdims=False)
    own_rank = lax.dynamic_index_in_dim(rank_in, vir, 1, keepdims=False)
    send_table = (
        jnp.arange(VIR, dtype=i32)[None, :, None] * VCAP
        + own_starts[:, :, None]
        + rank_in * own_counts[:, None, None]
    )
    which = lookup(local * VT + first, own_rank)
    position = lookup(local * NV + second, send_table) + which
    pick = jnp.arange(VIR * VCAP, dtype=i32)[:, None] == position[None, :]
    send = jnp.dot(pick.astype(jnp.bfloat16), t_tiles, preferred_element_type=jnp.float32).astype(jnp.bfloat16)
    across = lax.all_to_all(send.reshape(VIR, VCAP, AREA), "vir", split_axis=0, concat_axis=0, tiled=True)

    to_starts = lax.dynamic_index_in_dim(starts, vir, 2, keepdims=False)
    source = (jnp.arange(VIR, dtype=i32)[None, :] * VCAP + to_starts)[:, :, None] + rank_in
    source = jnp.arange(2, dtype=i32)[None, :, None, None] * counts[:, None, :, None] + source[:, None]
    at_rank = (rank_all.reshape(PAIRS, NV)[:, None, :] == jnp.arange(8, dtype=i32)[None, :, None]) & (
        mine.reshape(PAIRS, NV)[:, None, :] > 0
    )
    by_rank = jnp.sum(
        jnp.where(at_rank[:, None], source.reshape(PAIRS, 2, 1, NV), 0), axis=-1
    )
    alive = jnp.arange(2, dtype=i32)[None, :] < own_counts[:, None]
    by_rank = jnp.where(alive[:, :, None], by_rank, -1)
    own_map = lax.dynamic_slice_in_dim(cycle_map, occ * PAIRS, PAIRS, 0)
    to_group = own_map[None, :] == jnp.arange(OCC, dtype=i32)[:, None]
    by_group = jnp.sum(jnp.where(to_group[:, :, None], by_rank.reshape(1, PAIRS, 16), 0), axis=1)
    pick2 = by_group.reshape(-1)[:, None] == jnp.arange(VIR * VCAP, dtype=i32)[None, :]
    send2 = jnp.dot(
        pick2.astype(jnp.bfloat16), across.reshape(-1, AREA), preferred_element_type=jnp.float32
    ).astype(jnp.bfloat16)
    got = lax.all_to_all(send2.reshape(OCC, 16, AREA), "occ", split_axis=0, concat_axis=0, tiled=True)

    tile_key = (local * 2 + which) * NV + second
    row_key = (
        ladder_slots[:, 0][None, :] * 2 + jnp.arange(2, dtype=i32)[:, None]
    ) * NV + ladder_slots[:, 2][None, :]
    match = row_key[:, :, None] == tile_key[None, None, :]
    packed = jnp.arange(128, dtype=i32) * 8 + first + 1
    found = jnp.sum(jnp.where(match, packed, 0), axis=-1)
    ladder_tile = jnp.where(found > 0, (found - 1) // 8, 0)
    ladder_block = jnp.where(found > 0, ladder_slots[:, 1][None, :] * VT + (found - 1) % 8, BLOCKS)
    ladder_index = jnp.concatenate([ladder_block, ladder_tile], axis=0)
    ladder = rows_call(False, ladder_index, x_rows, t_tiles.reshape(128, TILE, TILE), "ladder")
    ladder_sum = lax.psum_scatter(ladder, "vir", scatter_dimension=0, tiled=True)

    owner = (cycle_map.reshape(OCC, PAIRS) == occ).astype(i32)
    owner_of = jnp.sum(owner * jnp.arange(OCC, dtype=i32)[:, None], axis=0)
    theirs = jnp.sum(owner[:, :, None, None] * domain, axis=0)
    counts_c, rank_in_c, rank_all_c = tables(theirs)
    here = lax.dynamic_index_in_dim(theirs, vir, 1, keepdims=False)
    here_rank = lax.dynamic_index_in_dim(rank_in_c, vir, 1, keepdims=False)
    ds = jnp.sum(
        jnp.where(
            (here_rank[:, None, :] == jnp.arange(2, dtype=i32)[None, :, None]) & (here[:, None, :] > 0),
            jnp.arange(1, VT + 1, dtype=i32),
            0,
        ),
        axis=-1,
    )
    s, a, b = cycle_slots[:, 0], cycle_slots[:, 1], cycle_slots[:, 2]
    rank_a = lookup(s * NV + a, rank_all_c)
    row_ds = lookup(s[None, :] * 2 + jnp.arange(2, dtype=i32)[:, None], ds)
    d = row_ds - 1
    cycle_block = ((b // 3) * 3 + d // 2) * 6 + (d % 2) * 3 + b % 3
    cycle_block = jnp.where(row_ds > 0, cycle_block, BLOCKS)
    cycle_tile = lookup(s, owner_of) * 16 + jnp.arange(2, dtype=i32)[:, None] * 8 + rank_a
    cycle_index = jnp.concatenate([cycle_block, cycle_tile], axis=0)
    cycle = rows_call(True, cycle_index, y_rows, got.reshape(256, TILE, TILE), "cycle")
    cycle_sum = lax.psum_scatter(cycle, "vir", scatter_dimension=0, tiled=True)

    def finish(octets):
        return octets.astype(jnp.float32).reshape(3, TILE, 8, TILE).transpose(0, 2, 1, 3).reshape(24, AREA)

    return finish(ladder_sum), finish(cycle_sum)


def solution(mesh):
    return jax.shard_map(
        on_device,
        mesh=mesh,
        in_specs=(
            P(("occ", "vir"), None),
            P(("occ", "vir"), None),
            P(),
            P("occ", None),
            P("occ", None),
            P("occ", "vir"),
            P("vir", "occ"),
        ),
        out_specs=(P(("occ", "vir"), None), P(("occ", "vir"), None)),
        check_vma=False,
    )
```

```python
import functools

import jax
import jax.numpy as jnp
from jax import lax
from jax.experimental import pallas as pl
from jax.experimental.pallas import tpu as pltpu
from jax.sharding import PartitionSpec as P

TILE = 96
NV = 48
AREA = TILE * TILE
OCC = 16
VIR = 8
VT = 6
PAIRS = 16
VCAP = 32
BLOCKS = 288
ROWS = 192
WIDE = 8 * TILE
H = 2
R = TILE // H
HALF = 144
MESH = pl.DeviceIdType.MESH
VPACK, OPACK, LADDER, CYCLE = 0, 256, 512, 512 + 4 * ROWS


def marks_kernel(mark_ref, out_ref, got, rows, table, send1, recv1, send2, recv2):
    occ, vir = lax.axis_index("occ"), lax.axis_index("vir")
    barrier = pltpu.get_barrier_semaphore()
    for k in range(1, VIR):
        pl.semaphore_signal(barrier, inc=1, device_id=(occ, (vir + k) % VIR), device_id_type=MESH)
    for k in range(1, OCC):
        pl.semaphore_signal(barrier, inc=1, device_id=((occ + k) % OCC, vir), device_id_type=MESH)
    pl.semaphore_wait(barrier, VIR + OCC - 2)
    copies = []
    for k in range(1, VIR):
        copy = pltpu.make_async_remote_copy(
            mark_ref, got.at[k - 1], send1.at[k - 1], recv1.at[k - 1],
            device_id=(occ, (vir + VIR - k) % VIR), device_id_type=MESH,
        )
        copy.start()
        copies.append(copy)
    line = lax.broadcasted_iota(jnp.int32, (8, 128), 0)
    all_rows = jnp.where(line == vir, mark_ref[...], 0)
    for k in range(1, VIR):
        copies[k - 1].wait_recv()
        all_rows = jnp.where(line == (vir + k) % VIR, got[k - 1], all_rows)
    rows[...] = all_rows
    for k in range(1, OCC):
        copy = pltpu.make_async_remote_copy(
            rows, table.at[k - 1], send2.at[k - 1], recv2.at[k - 1],
            device_id=((occ + OCC - k) % OCC, vir), device_id_type=MESH,
        )
        copy.start()
        copies.append(copy)
    out_ref[0] = all_rows
    for k in range(1, OCC):
        copies[VIR - 2 + k].wait_recv()
        out_ref[k] = table[k - 1]
    for copy in copies:
        copy.wait_send()


def marks_call(mark):
    return pl.pallas_call(
        marks_kernel,
        out_shape=jax.ShapeDtypeStruct((OCC, 8, 128), jnp.int32),
        in_specs=[pl.BlockSpec(memory_space=pltpu.VMEM)],
        out_specs=pl.BlockSpec(memory_space=pltpu.VMEM),
        scratch_shapes=[
            pltpu.VMEM((VIR - 1, 8, 128), jnp.int32),
            pltpu.VMEM((8, 128), jnp.int32),
            pltpu.VMEM((OCC - 1, 8, 128), jnp.int32),
            pltpu.SemaphoreType.DMA((VIR - 1,)),
            pltpu.SemaphoreType.DMA((VIR - 1,)),
            pltpu.SemaphoreType.DMA((OCC - 1,)),
            pltpu.SemaphoreType.DMA((OCC - 1,)),
        ],
        compiler_params=pltpu.CompilerParams(collective_id=0, has_side_effects=True),
        name="marks",
    )(mark)


def main_kernel(
    index_ref, t_ref, x_ref, y_ref, ladder_ref, cycle_ref,
    x_got, y_got, blocks, v_send, v_got, v_tiles, o_send, o_got, o_tiles,
    l_part, l_core, l_z, c_part, c_core, c_z,
    g_ss, g_rs, v_ss, v_rs, o_ss, o_rs, core_ss, core_rs, z_ss, z_rs,
):
    occ, vir = lax.axis_index("occ"), lax.axis_index("vir")
    ox, oy = occ // 4, occ % 4
    z, core = vir // 2, vir % 2
    barrier = pltpu.get_barrier_semaphore()
    for k in range(1, VIR):
        pl.semaphore_signal(barrier, inc=1, device_id=(occ, (vir + k) % VIR), device_id_type=MESH)
    for k in range(1, OCC):
        pl.semaphore_signal(barrier, inc=1, device_id=((occ + k) % OCC, vir), device_id_type=MESH)

    def v_pack(q, carry):
        for j in range(8):
            tile = t_ref[index_ref[VPACK + q * 8 + j]]
            for h in range(H):
                v_send[h, q // 4, q % 4, :, j * TILE : (j + 1) * TILE] = tile[h * R : (h + 1) * R]
        return carry

    lax.fori_loop(0, VIR * 4, v_pack, 0)
    pl.semaphore_wait(barrier, VIR + OCC - 2)
    sent = []

    def push(src, dst, ssem, rsem, device):
        copy = pltpu.make_async_remote_copy(src, dst, ssem, rsem, device_id=device, device_id_type=MESH)
        copy.start()
        sent.append(copy)
        return copy

    def v_push(h):
        return [
            push(v_send.at[h, k], v_got.at[h, VIR - k - 1], v_ss.at[h, k - 1], v_rs.at[h, VIR - k - 1],
                 (occ, (vir + k) % VIR))
            for k in range(1, VIR)
        ]

    shards = (x_ref, y_ref)
    landing = (x_got, y_got)

    def place(array, half, rel):
        rows = pl.ds(half * HALF, HALF)
        return shards[array].at[rows] if rel == 0 else landing[array].at[rel - 1, rows]

    def spread(array, half, along_y, rel, slot):
        copies = []
        dx, dy = rel // 4, rel % 4
        for k in (1, 3, 2):
            if along_y:
                target, there = (ox * 4 + (oy + k) % 4, vir), dx * 4 + (dy + 4 - k) % 4
            else:
                target, there = (((ox + k) % 4) * 4 + oy, vir), ((dx + 4 - k) % 4) * 4 + dy
            copies.append(push(
                place(array, half, rel), landing[array].at[there - 1, pl.ds(half * HALF, HALF)],
                g_ss.at[array, half, slot * 3 + k - 1], g_rs.at[array, half, there - 1], target,
            ))
        return copies

    stage1 = {}
    stage2 = {}

    def gather_start(array):
        for half in range(2):
            stage1[array, half] = spread(array, half, half == 0, 0, 0)
            stage2[array, half] = spread(array, half, half == 1, 0, 1)

    def gather_forward(array):
        for i, k in enumerate((1, 3, 2)):
            for half in range(2):
                stage1[array, half][i].wait_recv()
                rel = 4 - k if half == 0 else (4 - k) * 4
                stage2[array, half] = stage2[array, half] + spread(array, half, half == 1, rel, 1 + k)

    def gather_unpack(array):
        for half in range(2):
            for copy in stage2[array, half]:
                copy.wait_recv()

        def unpack_from(ref, base, n):
            for row in range(3):
                strip = ref[row * TILE : (row + 1) * TILE]
                for c in range(6):
                    blocks[base + row * 6 + c] = strip[:, c * TILE : (c + 1) * TILE]

        unpack_from(shards[array], 0, 3)

        def body(n, carry):
            unpack_from(landing[array].at[n], (n + 1) * 18, 3)
            return carry

        lax.fori_loop(0, OCC - 1, body, 0)

    gather_start(0)
    v_copies = [v_push(h) for h in range(H)]
    gather_start(1)
    blocks[BLOCKS] = jnp.zeros((TILE, TILE), jnp.bfloat16)
    gather_forward(0)
    gather_forward(1)

    def split(dst, strip, base):
        for j in range(8):
            dst[base + j] = strip[:, j * TILE : (j + 1) * TILE]

    def o_step(h):
        for copy in v_copies[h]:
            copy.wait_recv()
        for q in range(4):
            split(v_tiles, v_send[h, 0, q], q * 8)

        def unpack(q, carry):
            split(v_tiles, v_got[h, q // 4, q % 4], (q + 4) * 8)
            return carry

        lax.fori_loop(0, (VIR - 1) * 4, unpack, 0)

        def pack(q, carry):
            for j in range(8):
                o_send[h, q // 2, q % 2, :, j * TILE : (j + 1) * TILE] = v_tiles[index_ref[OPACK + q * 8 + j]]
            return carry

        lax.fori_loop(0, OCC * 2, pack, 0)
        return [
            push(o_send.at[h, k], o_got.at[h, OCC - k - 1], o_ss.at[h, k - 1], o_rs.at[h, OCC - k - 1],
                 ((occ + k) % OCC, vir))
            for k in range(1, OCC)
        ]

    def products(base, tiles, part, swap):
        def octet(q, carry):
            owner = q // 3
            for j in range(8):
                row = q * 8 + j
                total = None
                for half in range(2):
                    block = blocks[index_ref[base + half * ROWS + row]]
                    tile = tiles[index_ref[base + (2 + half) * ROWS + row]]
                    left, right = (tile, block) if swap else (block, tile)
                    term = jnp.dot(left, right, preferred_element_type=jnp.float32)
                    total = term if total is None else total + term
                part[owner % 2, owner // 2, q % 3, :, j * TILE : (j + 1) * TILE] = total.astype(jnp.bfloat16)
            return carry

        lax.fori_loop(0, ROWS // 8, octet, 0)

    def core_push(n, part, dst):
        return push(part.at[1 - core], dst, core_ss.at[n], core_rs.at[n], (occ, z * 2 + 1 - core))

    def z_push(n, copy, part, dst, z_got):
        copy.wait_recv()

        def add(q, carry):
            total = part[core, q // 3, q % 3].astype(jnp.float32) + dst[q // 3, q % 3].astype(jnp.float32)
            dst[q // 3, q % 3] = total.astype(jnp.bfloat16)
            return carry

        lax.fori_loop(0, 12, add, 0)
        return [
            push(dst.at[(z + k) % 4], z_got.at[4 - k - 1], z_ss.at[n, k - 1], z_rs.at[n, 4 - k - 1],
                 (occ, ((z + k) % 4) * 2 + core))
            for k in (1, 3, 2)
        ]

    def finish(copies, dst, z_got, out, first, rows):
        for copy in copies:
            copy.wait_recv()
        for i in range(3):
            total = dst[z, i].astype(jnp.float32)
            for k in range(3):
                total = total + z_got[k, i].astype(jnp.float32)
            out[i, first : first + rows] = total

    o_copies = [o_step(h) for h in range(H)]
    gather_unpack(0)
    products(LADDER, t_ref, l_part, False)
    l_copy = core_push(H, l_part, l_core)
    gather_unpack(1)
    l_copies = z_push(H, l_copy, l_part, l_core, l_z)
    c_copies = []
    for h in range(H):
        for copy in o_copies[h]:
            copy.wait_recv()
        for j in range(2):
            split(o_tiles, o_send[h, 0, j], j * 8)

        def unpack(q, carry):
            split(o_tiles, o_got[h, q // 2, q % 2], (q + 2) * 8)
            return carry

        lax.fori_loop(0, (OCC - 1) * 2, unpack, 0)
        products(CYCLE, o_tiles, c_part.at[h], True)
        c_copies.append(core_push(h, c_part.at[h], c_core.at[h]))
        if h > 0:
            c_copies[h - 1] = z_push(h - 1, c_copies[h - 1], c_part.at[h - 1], c_core.at[h - 1], c_z.at[h - 1])
    c_copies[H - 1] = z_push(H - 1, c_copies[H - 1], c_part.at[H - 1], c_core.at[H - 1], c_z.at[H - 1])
    finish(l_copies, l_core, l_z, ladder_ref, 0, TILE)
    for h in range(H):
        finish(c_copies[h], c_core.at[h], c_z.at[h], cycle_ref, h * R, R)
    for copy in sent:
        copy.wait_send()


def main_call(index, tiles, x, y):
    bf16 = jnp.bfloat16
    vmem = pl.BlockSpec(memory_space=pltpu.VMEM)
    dma = pltpu.SemaphoreType.DMA
    out = jax.ShapeDtypeStruct((3, TILE, WIDE), jnp.float32)
    return pl.pallas_call(
        main_kernel,
        out_shape=(out, out),
        in_specs=[pl.BlockSpec(memory_space=pltpu.SMEM), vmem, vmem, vmem],
        out_specs=(vmem, vmem),
        scratch_shapes=[
            pltpu.VMEM((OCC - 1, 3 * TILE, 6 * TILE), bf16),
            pltpu.VMEM((OCC - 1, 3 * TILE, 6 * TILE), bf16),
            pltpu.VMEM((BLOCKS + 1, TILE, TILE), bf16),
            pltpu.VMEM((H, VIR, 4, R, WIDE), bf16),
            pltpu.VMEM((H, VIR - 1, 4, R, WIDE), bf16),
            pltpu.VMEM((256, R, TILE), bf16),
            pltpu.VMEM((H, OCC, 2, R, WIDE), bf16),
            pltpu.VMEM((H, OCC - 1, 2, R, WIDE), bf16),
            pltpu.VMEM((256, R, TILE), bf16),
            pltpu.VMEM((2, 4, 3, TILE, WIDE), bf16),
            pltpu.VMEM((4, 3, TILE, WIDE), bf16),
            pltpu.VMEM((3, 3, TILE, WIDE), bf16),
            pltpu.VMEM((H, 2, 4, 3, R, WIDE), bf16),
            pltpu.VMEM((H, 4, 3, R, WIDE), bf16),
            pltpu.VMEM((H, 3, 3, R, WIDE), bf16),
            dma((2, 2, 15)), dma((2, 2, 15)),
            dma((H, VIR - 1)), dma((H, VIR - 1)),
            dma((H, OCC - 1)), dma((H, OCC - 1)),
            dma((H + 1,)), dma((H + 1,)),
            dma((H + 1, 3)), dma((H + 1, 3)),
        ],
        compiler_params=pltpu.CompilerParams(
            collective_id=1, has_side_effects=True, vmem_limit_bytes=63_000_000
        ),
        cost_estimate=pl.CostEstimate(flops=8 * ROWS * TILE**3, bytes_accessed=14_000_000, transcendentals=0),
        name="contract",
    )(index, tiles, x, y)


def lookup(ids, table):
    flat = table.reshape(-1)
    hits = ids[..., None] == jnp.arange(flat.shape[0], dtype=jnp.int32)
    return jnp.sum(jnp.where(hits, flat, 0), axis=-1)


def before(counts, axis):
    return jnp.cumsum(counts, axis=axis) - counts


def on_device(t_tiles, t_index, cycle_map, ladder_slots, cycle_slots, x_ints, y_ints):
    occ = lax.axis_index("occ")
    vir = lax.axis_index("vir")
    i32 = jnp.int32
    local = t_index[:, 0] - occ * PAIRS
    first = t_index[:, 1] - vir * VT
    second = t_index[:, 2]
    pair_range = jnp.arange(2, dtype=i32)
    vir_range = jnp.arange(VIR, dtype=i32)

    marks = jnp.arange(128, dtype=i32)[None, :] == (local * VT + first)[:, None]
    held = jnp.max(marks.astype(i32), axis=0)
    table = marks_call(jnp.broadcast_to(held[None], (8, 128)))
    domain = table[:, :, : PAIRS * VT].reshape(OCC, VIR, PAIRS, VT).transpose(0, 2, 1, 3)

    def tables(dom):
        counts = jnp.sum(dom, axis=-1)
        rank_in = before(dom, 2)
        rank_all = rank_in + before(counts, 1)[..., None]
        return counts, rank_in, rank_all

    mine = domain[0]
    counts, rank_in, rank_all = tables(mine)
    starts = before(counts[:, :, None] * counts[:, None, :], 0)

    own_counts = lax.dynamic_index_in_dim(counts, vir, 1, keepdims=False)
    own_starts = lax.dynamic_index_in_dim(starts, vir, 1, keepdims=False)
    own_rank = lax.dynamic_index_in_dim(rank_in, vir, 1, keepdims=False)
    send_table = (
        ((vir_range - vir) % VIR)[None, :, None] * VCAP
        + own_starts[:, :, None]
        + rank_in * own_counts[:, None, None]
    )
    which = lookup(local * VT + first, own_rank)
    position = lookup(local * NV + second, send_table) + which
    pick = jnp.arange(VIR * VCAP, dtype=i32)[:, None] == position[None, :]
    v_pack = jnp.sum(jnp.where(pick, jnp.arange(128, dtype=i32), 0), axis=1)

    to_starts = lax.dynamic_index_in_dim(starts, vir, 2, keepdims=False)
    source = (((vir_range - vir) % VIR)[None, :] * VCAP + to_starts)[:, :, None] + rank_in
    source = pair_range[None, :, None, None] * counts[:, None, :, None] + source[:, None]
    at_rank = (rank_all.reshape(PAIRS, NV)[:, None, :] == jnp.arange(8, dtype=i32)[None, :, None]) & (
        mine.reshape(PAIRS, NV)[:, None, :] > 0
    )
    by_rank = jnp.sum(jnp.where(at_rank[:, None], source.reshape(PAIRS, 2, 1, NV), 0), axis=-1)
    alive = pair_range[None, :] < own_counts[:, None]
    by_rank = jnp.where(alive[:, :, None], by_rank, 0)
    own_map = lax.dynamic_slice_in_dim(cycle_map, occ * PAIRS, PAIRS, 0)
    to_group = own_map[None, :] == ((occ + jnp.arange(OCC, dtype=i32)) % OCC)[:, None]
    o_pack = jnp.sum(jnp.where(to_group[:, :, None], by_rank.reshape(1, PAIRS, 16), 0), axis=1)

    def ahead(group):
        return ((group // 4 - occ // 4) % 4) * 4 + (group % 4 - occ % 4) % 4

    tile_key = (local * 2 + which) * NV + second
    row_key = (ladder_slots[:, 0][None, :] * 2 + pair_range[:, None]) * NV + ladder_slots[:, 2][None, :]
    match = row_key[:, :, None] == tile_key[None, None, :]
    packed = jnp.arange(128, dtype=i32) * 8 + first + 1
    found = jnp.sum(jnp.where(match, packed, 0), axis=-1)
    ladder_tile = jnp.where(found > 0, (found - 1) // 8, 0)
    x_row = ladder_slots[:, 1]
    x_block = (ahead(x_row // 3) * 3 + x_row % 3) * VT
    ladder_block = jnp.where(found > 0, x_block[None, :] + (found - 1) % 8, BLOCKS)

    by_o = (cycle_map.reshape(OCC, PAIRS) == occ).astype(i32)
    ahead_of = jnp.sum(by_o * ((jnp.arange(OCC, dtype=i32) - occ) % OCC)[:, None], axis=0)
    owner = (jnp.arange(OCC, dtype=i32)[:, None] == ahead_of[None, :]).astype(i32)
    theirs = jnp.sum(owner[:, :, None, None] * domain, axis=0)
    _, rank_in_c, rank_all_c = tables(theirs)
    here = lax.dynamic_index_in_dim(theirs, vir, 1, keepdims=False)
    here_rank = lax.dynamic_index_in_dim(rank_in_c, vir, 1, keepdims=False)
    ds = jnp.sum(
        jnp.where(
            (here_rank[:, None, :] == pair_range[None, :, None]) & (here[:, None, :] > 0),
            jnp.arange(1, VT + 1, dtype=i32),
            0,
        ),
        axis=-1,
    )
    s, a, b = cycle_slots[:, 0], cycle_slots[:, 1], cycle_slots[:, 2]
    rank_a = lookup(s * NV + a, rank_all_c)
    row_ds = lookup(s[None, :] * 2 + pair_range[:, None], ds)
    d = row_ds - 1
    cycle_block = (ahead(b // 3) * 3 + d // 2) * 6 + (d % 2) * 3 + b % 3
    cycle_block = jnp.where(row_ds > 0, cycle_block, BLOCKS)
    cycle_tile = lookup(s, ahead_of) * 16 + pair_range[:, None] * 8 + rank_a
    index = jnp.concatenate(
        [v_pack, o_pack.reshape(-1)]
        + [rows.reshape(-1) for rows in (ladder_block, ladder_tile, cycle_block, cycle_tile)]
    )
    y_pack = y_ints.reshape(3, 2, TILE, 3, TILE).transpose(0, 2, 1, 3, 4).reshape(3 * TILE, 6 * TILE)
    ladder, cycle = main_call(index, t_tiles.reshape(128, TILE, TILE), x_ints, y_pack)

    def finish(octets):
        return octets.reshape(3, TILE, 8, TILE).transpose(0, 2, 1, 3).reshape(24, AREA)

    return finish(ladder), finish(cycle)


def solution(mesh):
    return jax.shard_map(
        on_device,
        mesh=mesh,
        in_specs=(
            P(("occ", "vir"), None),
            P(("occ", "vir"), None),
            P(),
            P("occ", None),
            P("occ", None),
            P("occ", "vir"),
            P("vir", "occ"),
        ),
        out_specs=(P(("occ", "vir"), None), P(("occ", "vir"), None)),
        check_vma=False,
    )
```

```python
import functools

import jax
import jax.numpy as jnp
from jax import lax
from jax.experimental import pallas as pl
from jax.experimental.pallas import tpu as pltpu
from jax.sharding import PartitionSpec as P

TILE = 96
NV = 48
AREA = TILE * TILE
OCC = 16
VIR = 8
VT = 6
PAIRS = 16
VCAP = 32
BLOCKS = 288
ROWS = 192
WIDE = 8 * TILE
H = 2
R = TILE // H
FLAT = 144
SUBS = ((0, 80), (80, 64))
MESH = pl.DeviceIdType.MESH
VPACK, LADDER = 0, 256


def main_kernel(
    index_ref, label_ref, rows_ref, t_ref, x_ref, y_ref, ladder_ref, cycle_ref,
    x_got, y_got, blocks, v_send, v_got, v_tiles, o_send, o_got, o_tiles,
    l_part, l_core, l_z, c_part, c_core, c_z,
    v_label, o_label, o_label_got, words, o_index, c_index,
    g_ss, g_rs, v_ss, v_rs, o_ss, o_rs, core_ss, core_rs, z_ss, z_rs,
    vl_ss, vl_rs, ol_ss, ol_rs, w_sem,
):
    occ, vir = lax.axis_index("occ"), lax.axis_index("vir")
    ox, oy = occ // 4, occ % 4
    z, core = vir // 2, vir % 2
    i32 = jnp.int32
    barrier = pltpu.get_barrier_semaphore()
    for k in range(1, VIR):
        pl.semaphore_signal(barrier, inc=1, device_id=(occ, (vir + k) % VIR), device_id_type=MESH)
    for k in range(1, OCC):
        pl.semaphore_signal(barrier, inc=1, device_id=((occ + k) % OCC, vir), device_id_type=MESH)

    pl.semaphore_wait(barrier, VIR + OCC - 2)
    sent = []

    def push(src, dst, ssem, rsem, device):
        copy = pltpu.make_async_remote_copy(src, dst, ssem, rsem, device_id=device, device_id_type=MESH)
        copy.start()
        sent.append(copy)
        return copy

    shards = (x_ref, y_ref)
    landing = (x_got, y_got)
    count = [0, 0]

    def step(rel, axis, k):
        dx, dy = rel // 4, rel % 4
        return ((dx - k) % 4) * 4 + dy if axis == 0 else dx * 4 + (dy - k) % 4

    def target(axis, k):
        return (((ox + k) % 4) * 4 + oy, vir) if axis == 0 else (ox * 4 + (oy + k) % 4, vir)

    def send_sem(array):
        count[array] += 1
        return g_ss.at[array, count[array] - 1]

    def spread(array, axis, rel):
        source = shards[array] if rel == 0 else landing[array].at[rel - 1]
        copies = {}
        for k in (1, 3):
            there = step(rel, axis, k)
            copies[k] = push(
                source, landing[array].at[there - 1], send_sem(array), g_rs.at[array, there - 1, 0], target(axis, k)
            )
        return copies

    def forward(array, axis, rel, copies, flip):
        out = []
        for n, k in enumerate((1, 3)):
            copies[k].wait_recv()
            here = step(rel, axis, k)
            there = step(here, axis, k)
            which = (n + flip) % 2
            rows = pl.ds(*SUBS[which])
            out.append(push(
                landing[array].at[here - 1, rows], landing[array].at[there - 1, rows],
                send_sem(array), g_rs.at[array, there - 1, which], target(axis, k),
            ))
        return out

    first_axis, second_axis = (1, 0), (0, 1)
    first = [spread(array, first_axis[array], 0) for array in range(2)]
    v_labels = [
        push(label_ref.at[k], v_label.at[VIR - k - 1], vl_ss.at[k - 1], vl_rs.at[VIR - k - 1], (occ, (vir + k) % VIR))
        for k in range(1, VIR)
    ]
    second = [{0: spread(array, second_axis[array], 0)} for array in range(2)]
    turned = [[], []]

    def v_pack(q, carry):
        for j in range(8):
            tile = t_ref[index_ref[VPACK + q * 8 + j]]
            for h in range(H):
                v_send[h, q // 4, q % 4, :, j * TILE : (j + 1) * TILE] = tile[h * R : (h + 1) * R]
        return carry

    lax.fori_loop(0, VIR * 4, v_pack, 0)

    def v_push(h):
        return [
            push(v_send.at[h, k], v_got.at[h, VIR - k - 1], v_ss.at[h, k - 1], v_rs.at[h, VIR - k - 1],
                 (occ, (vir + k) % VIR))
            for k in range(1, VIR)
        ]

    v_copies = [v_push(h) for h in range(H)]

    middle = [forward(array, first_axis[array], 0, first[array], 0) for array in range(2)]
    for k in (1, 3):
        for array in range(2):
            rel = step(0, first_axis[array], k)
            second[array][rel] = spread(array, second_axis[array], rel)

    line = lax.broadcasted_iota(i32, (VCAP, 128), 0)
    lane = lax.broadcasted_iota(i32, (VCAP, 128), 1)
    places = [jnp.zeros((VCAP, 128), i32)] * 2
    infos = [jnp.zeros((VCAP, 128), i32)] * 2
    for k in range(VIR):
        if k == 0:
            label = label_ref[0]
        else:
            v_labels[VIR - k - 1].wait_recv()
            label = v_label[k - 1]
        for half in range(2):
            hit = (label >= 0) & ((label & 255) == lane + 128 * half)
            places[half] = places[half] + jnp.where(hit, line + k * VCAP, 0)
            infos[half] = infos[half] + jnp.where(hit, (label >> 8) + 1, 0)
    words[...] = jnp.zeros((16, 128), i32)
    for half in range(2):
        words[half : half + 1] = jnp.minimum(jnp.sum(places[half], axis=0, keepdims=True), VIR * VCAP - 1)
        info = jnp.sum(infos[half].astype(jnp.float32), axis=0, keepdims=True)
        column = jnp.transpose(jnp.broadcast_to(info, (128, 128))).astype(i32)
        o_label[half * 8 : half * 8 + 8] = column.reshape(8, 16, 128)
    to_scalar = pltpu.make_async_copy(words.at[0:8], o_index, w_sem.at[0])
    to_scalar.start()
    o_labels = [
        push(o_label.at[k], o_label_got.at[OCC - k - 1], ol_ss.at[k - 1], ol_rs.at[OCC - k - 1], ((occ + k) % OCC, vir))
        for k in range(1, OCC)
    ]
    to_scalar.wait()

    for array in range(2):
        for copy in middle[array]:
            copy.wait_recv()
        rel = step(step(0, first_axis[array], 1), first_axis[array], 1)
        second[array][rel] = spread(array, second_axis[array], rel)
    blocks[BLOCKS] = jnp.zeros((TILE, TILE), jnp.bfloat16)
    for n in range(4):
        for array in range(2):
            rel = list(second[array])[n]
            turned[array] = turned[array] + forward(array, second_axis[array], rel, second[array][rel], n % 2)

    def gather_unpack(array):
        for copy in turned[array]:
            copy.wait_recv()

        def unpack_from(ref, base):
            left, right = ref[:, : 6 * TILE], ref[:, 6 * TILE :]
            strips = (left[:TILE], jnp.concatenate([left[TILE:], right[: 2 * TILE - FLAT]], axis=0), right[2 * TILE - FLAT :])
            for row in range(3):
                for c in range(6):
                    blocks[base + row * 6 + c] = strips[row][:, c * TILE : (c + 1) * TILE]

        unpack_from(shards[array], 0)

        def body(n, carry):
            unpack_from(landing[array].at[n], (n + 1) * 18)
            return carry

        lax.fori_loop(0, OCC - 1, body, 0)

    def cycle_words():
        line16 = lax.broadcasted_iota(i32, (16, 128), 0)
        totals = [jnp.zeros((16, 128), i32)] * 2
        for k in range(OCC):
            if k == 0:
                label = o_label[0]
            else:
                o_labels[OCC - k - 1].wait_recv()
                label = o_label_got[k - 1]
            value = (line16 + k * 16) * 8 + ((label - 1) & 7) + 1
            for half in range(2):
                hit = (label > 0) & (rows_ref[half, 0:1] == k) & (((label - 1) >> 3) == rows_ref[half, 1:2])
                totals[half] = totals[half] + jnp.where(hit, value, 0)
        for half in range(2):
            for j in range(2):
                found = jnp.sum(totals[half][j * 8 : j * 8 + 8], axis=0, keepdims=True)
                block = jnp.where(found > 0, rows_ref[half, 2:3] + 3 * ((found - 1) & 7), BLOCKS)
                tile = jnp.where(found > 0, (found - 1) >> 3, 0)
                words[8 + half * 4 + j : 9 + half * 4 + j] = jnp.clip(block, 0, BLOCKS)
                words[10 + half * 4 + j : 11 + half * 4 + j] = jnp.minimum(tile, 255)
        copy = pltpu.make_async_copy(words.at[8:16], c_index, w_sem.at[1])
        copy.start()
        copy.wait()

    def split(dst, strip, base):
        for j in range(8):
            dst[base + j] = strip[:, j * TILE : (j + 1) * TILE]

    def o_step(h):
        for copy in v_copies[h]:
            copy.wait_recv()
        for q in range(4):
            split(v_tiles, v_send[h, 0, q], q * 8)

        def unpack(q, carry):
            split(v_tiles, v_got[h, q // 4, q % 4], (q + 4) * 8)
            return carry

        lax.fori_loop(0, (VIR - 1) * 4, unpack, 0)

        def pack(q, carry):
            for j in range(8):
                o_send[h, q // 2, q % 2, :, j * TILE : (j + 1) * TILE] = v_tiles[o_index[q // 16, (q % 16) * 8 + j]]
            return carry

        lax.fori_loop(0, OCC * 2, pack, 0)
        return [
            push(o_send.at[h, k], o_got.at[h, OCC - k - 1], o_ss.at[h, k - 1], o_rs.at[h, OCC - k - 1],
                 ((occ + k) % OCC, vir))
            for k in range(1, OCC)
        ]

    def products(look, tiles, part, swap):
        def octet(q, carry):
            owner = q // 3
            for j in range(8):
                row = q * 8 + j
                total = None
                for half in range(2):
                    block = blocks[look(half, row)]
                    tile = tiles[look(2 + half, row)]
                    left, right = (tile, block) if swap else (block, tile)
                    term = jnp.dot(left, right, preferred_element_type=jnp.float32)
                    total = term if total is None else total + term
                part[owner % 2, owner // 2, q % 3, :, j * TILE : (j + 1) * TILE] = total.astype(jnp.bfloat16)
            return carry

        lax.fori_loop(0, ROWS // 8, octet, 0)

    def core_push(n, part, dst):
        return push(part.at[1 - core], dst, core_ss.at[n], core_rs.at[n], (occ, z * 2 + 1 - core))

    def z_push(n, copy, part, dst, z_got):
        copy.wait_recv()

        def add(q, carry):
            total = part[core, q // 3, q % 3].astype(jnp.float32) + dst[q // 3, q % 3].astype(jnp.float32)
            dst[q // 3, q % 3] = total.astype(jnp.bfloat16)
            return carry

        lax.fori_loop(0, 12, add, 0)
        return [
            push(dst.at[(z + k) % 4], z_got.at[4 - k - 1], z_ss.at[n, k - 1], z_rs.at[n, 4 - k - 1],
                 (occ, ((z + k) % 4) * 2 + core))
            for k in (1, 3, 2)
        ]

    def finish(copies, dst, z_got, out, first, rows):
        for copy in copies:
            copy.wait_recv()
        for i in range(3):
            total = dst[z, i].astype(jnp.float32)
            for k in range(3):
                total = total + z_got[k, i].astype(jnp.float32)
            out[i, first : first + rows] = total

    o_copies = [o_step(h) for h in range(H)]
    gather_unpack(0)
    products(lambda n, row: index_ref[LADDER + n * ROWS + row], t_ref, l_part, False)
    l_copy = core_push(H, l_part, l_core)
    cycle_words()
    gather_unpack(1)
    l_copies = z_push(H, l_copy, l_part, l_core, l_z)
    c_copies = []
    for h in range(H):
        for copy in o_copies[h]:
            copy.wait_recv()
        for j in range(2):
            split(o_tiles, o_send[h, 0, j], j * 8)

        def unpack(q, carry):
            split(o_tiles, o_got[h, q // 2, q % 2], (q + 2) * 8)
            return carry

        lax.fori_loop(0, (OCC - 1) * 2, unpack, 0)
        products(lambda n, row: c_index[(row // 128) * 4 + n, row % 128], o_tiles, c_part.at[h], True)
        c_copies.append(core_push(h, c_part.at[h], c_core.at[h]))
        if h > 0:
            c_copies[h - 1] = z_push(h - 1, c_copies[h - 1], c_part.at[h - 1], c_core.at[h - 1], c_z.at[h - 1])
    c_copies[H - 1] = z_push(H - 1, c_copies[H - 1], c_part.at[H - 1], c_core.at[H - 1], c_z.at[H - 1])
    finish(l_copies, l_core, l_z, ladder_ref, 0, TILE)
    for h in range(H):
        finish(c_copies[h], c_core.at[h], c_z.at[h], cycle_ref, h * R, R)
    for copy in sent:
        copy.wait_send()


def main_call(index, labels, rows, tiles, x, y):
    bf16 = jnp.bfloat16
    vmem = pl.BlockSpec(memory_space=pltpu.VMEM)
    dma = pltpu.SemaphoreType.DMA
    out = jax.ShapeDtypeStruct((3, TILE, WIDE), jnp.float32)
    return pl.pallas_call(
        main_kernel,
        out_shape=(out, out),
        in_specs=[pl.BlockSpec(memory_space=pltpu.SMEM)] + [vmem] * 5,
        out_specs=(vmem, vmem),
        scratch_shapes=[
            pltpu.VMEM((OCC - 1, FLAT, 12 * TILE), bf16),
            pltpu.VMEM((OCC - 1, FLAT, 12 * TILE), bf16),
            pltpu.VMEM((BLOCKS + 1, TILE, TILE), bf16),
            pltpu.VMEM((H, VIR, 4, R, WIDE), bf16),
            pltpu.VMEM((H, VIR - 1, 4, R, WIDE), bf16),
            pltpu.VMEM((256, R, TILE), bf16),
            pltpu.VMEM((H, OCC, 2, R, WIDE), bf16),
            pltpu.VMEM((H, OCC - 1, 2, R, WIDE), bf16),
            pltpu.VMEM((256, R, TILE), bf16),
            pltpu.VMEM((2, 4, 3, TILE, WIDE), bf16),
            pltpu.VMEM((4, 3, TILE, WIDE), bf16),
            pltpu.VMEM((3, 3, TILE, WIDE), bf16),
            pltpu.VMEM((H, 2, 4, 3, R, WIDE), bf16),
            pltpu.VMEM((H, 4, 3, R, WIDE), bf16),
            pltpu.VMEM((H, 3, 3, R, WIDE), bf16),
            pltpu.VMEM((VIR - 1, VCAP, 128), jnp.int32),
            pltpu.VMEM((OCC, 16, 128), jnp.int32),
            pltpu.VMEM((OCC - 1, 16, 128), jnp.int32),
            pltpu.VMEM((16, 128), jnp.int32),
            pltpu.SMEM((8, 128), jnp.int32),
            pltpu.SMEM((8, 128), jnp.int32),
            dma((2, 20)), dma((2, OCC - 1, 2)),
            dma((H, VIR - 1)), dma((H, VIR - 1)),
            dma((H, OCC - 1)), dma((H, OCC - 1)),
            dma((H + 1,)), dma((H + 1,)),
            dma((H + 1, 3)), dma((H + 1, 3)),
            dma((VIR - 1,)), dma((VIR - 1,)), dma((OCC - 1,)), dma((OCC - 1,)), dma((2,)),
        ],
        compiler_params=pltpu.CompilerParams(
            collective_id=1, has_side_effects=True, vmem_limit_bytes=63_000_000
        ),
        cost_estimate=pl.CostEstimate(flops=8 * ROWS * TILE**3, bytes_accessed=14_000_000, transcendentals=0),
        name="contract",
    )(index, labels, rows, tiles, x, y)


def lookup(ids, table):
    flat = table.reshape(-1)
    hits = ids[..., None] == jnp.arange(flat.shape[0], dtype=jnp.int32)
    return jnp.sum(jnp.where(hits, flat, 0), axis=-1)


def before(counts, axis):
    return jnp.cumsum(counts, axis=axis) - counts


def on_device(t_tiles, t_index, cycle_map, ladder_slots, cycle_slots, x_ints, y_ints):
    occ = lax.axis_index("occ")
    vir = lax.axis_index("vir")
    i32 = jnp.int32
    local = t_index[:, 0] - occ * PAIRS
    first = t_index[:, 1] - vir * VT
    second = t_index[:, 2]
    pair_range = jnp.arange(2, dtype=i32)
    vir_range = jnp.arange(VIR, dtype=i32)

    marks = jnp.arange(PAIRS * NV, dtype=i32)[None, :] == (local * NV + second)[:, None]
    domain = jnp.max(marks.astype(i32), axis=0).reshape(PAIRS, VIR, VT)
    counts = jnp.sum(domain, axis=-1)
    rank_in = before(domain, 2)
    rank_all = rank_in + before(counts, 1)[..., None]
    own_counts = lax.dynamic_index_in_dim(counts, vir, 1, keepdims=True)
    starts = before(own_counts * counts, 0)

    send_table = ((vir_range - vir) % VIR)[None, :, None] * VCAP + starts[:, :, None] + rank_in * own_counts[:, :, None]
    by_second = lookup(local * NV + second, send_table * 2 + rank_in)
    to_group = (lax.dynamic_slice_in_dim(cycle_map, occ * PAIRS, PAIRS, 0) - occ) % OCC
    own_rank = lax.dynamic_index_in_dim(rank_in, vir, 1, keepdims=False)
    own_all = lax.dynamic_index_in_dim(rank_all, vir, 1, keepdims=False)
    by_first = lookup(local * VT + first, own_rank + 2 * own_all + 16 * to_group[:, None])
    which = by_first % 2
    position = by_second // 2 + which
    target = (by_first // 16) * 16 + (by_second % 2) * 8 + (by_first // 2) % 8
    label = target + 256 * (t_index[:, 1] * 8 + second % VT)
    pick = jnp.arange(VIR * VCAP, dtype=i32)[:, None] == position[None, :]
    packed_pick = jnp.sum(jnp.where(pick, label * 128 + jnp.arange(128, dtype=i32) + 1, 0), axis=1)
    v_pack = jnp.where(packed_pick > 0, (packed_pick - 1) % 128, 0)
    labels = jnp.where(packed_pick > 0, (packed_pick - 1) // 128, -1)
    labels = jnp.broadcast_to(labels.reshape(VIR, VCAP, 1), (VIR, VCAP, 128))

    def ahead(group):
        return ((group // 4 - occ // 4) % 4) * 4 + (group % 4 - occ % 4) % 4

    tile_key = (local * 2 + which) * NV + second
    row_key = (ladder_slots[:, 0][None, :] * 2 + pair_range[:, None]) * NV + ladder_slots[:, 2][None, :]
    match = row_key[:, :, None] == tile_key[None, None, :]
    packed = jnp.arange(128, dtype=i32) * 8 + first + 1
    found = jnp.sum(jnp.where(match, packed, 0), axis=-1)
    ladder_tile = jnp.where(found > 0, (found - 1) // 8, 0)
    x_row = ladder_slots[:, 1]
    x_block = (ahead(x_row // 3) * 3 + x_row % 3) * VT
    ladder_block = jnp.where(found > 0, x_block[None, :] + (found - 1) % 8, BLOCKS)

    by_o = (cycle_map.reshape(OCC, PAIRS) == occ).astype(i32)
    ahead_of = jnp.sum(by_o * ((jnp.arange(OCC, dtype=i32) - occ) % OCC)[:, None], axis=0)
    s, a, b = cycle_slots[:, 0], cycle_slots[:, 1], cycle_slots[:, 2]
    rows = jnp.stack([lookup(s, ahead_of), a, ahead(b // 3) * 18 + b % 3], axis=0)
    rows = jnp.pad(rows, ((0, 5), (0, 256 - ROWS)), constant_values=-1).reshape(8, 2, 128).transpose(1, 0, 2)

    index = jnp.concatenate([v_pack, ladder_block.reshape(-1), ladder_tile.reshape(-1)])
    x_flat = jnp.concatenate([x_ints[:FLAT], x_ints[FLAT:]], axis=1)
    y_rows = y_ints.reshape(3, 2, TILE, 3, TILE).transpose(0, 2, 1, 3, 4).reshape(3 * TILE, 6 * TILE)
    y_flat = jnp.concatenate([y_rows[:FLAT], y_rows[FLAT:]], axis=1)
    ladder, cycle = main_call(index, labels, rows, t_tiles.reshape(128, TILE, TILE), x_flat, y_flat)

    def finish(octets):
        return octets.reshape(3, TILE, 8, TILE).transpose(0, 2, 1, 3).reshape(24, AREA)

    return finish(ladder), finish(cycle)


def solution(mesh):
    return jax.shard_map(
        on_device,
        mesh=mesh,
        in_specs=(
            P(("occ", "vir"), None),
            P(("occ", "vir"), None),
            P(),
            P("occ", None),
            P("occ", None),
            P("occ", "vir"),
            P("vir", "occ"),
        ),
        out_specs=(P(("occ", "vir"), None), P(("occ", "vir"), None)),
        check_vma=False,
    )
```

```python
import functools

import jax
import jax.numpy as jnp
from jax import lax
from jax.experimental import pallas as pl
from jax.experimental.pallas import tpu as pltpu
from jax.sharding import PartitionSpec as P

TILE = 96
NV = 48
AREA = TILE * TILE
OCC = 16
VIR = 8
VT = 6
PAIRS = 16
VCAP = 32
BLOCKS = 288
ROWS = 192
WIDE = 8 * TILE
CHUNKS = ((0, 32), (32, 32), (64, 32))
H = len(CHUNKS)
MOST = max(n for _, n in CHUNKS)
FLAT = 144
SUBS = ((0, 80), (80, 64))
MESH = pl.DeviceIdType.MESH
VPACK, LADDER = 0, 256


def main_kernel(
    index_ref, label_ref, rows_ref, t_ref, x_ref, y_ref, ladder_ref, cycle_ref,
    x_flat, y_flat, x_got, y_got, blocks, v_send, v_got, o_send, o_got, small,
    l_part, l_core, l_z, c_part, c_core, c_z,
    v_label, o_label, o_label_got, words, o_index, c_index,
    g_ss, g_rs, v_ss, v_rs, o_ss, o_rs, core_ss, core_rs, z_ss, z_rs,
    vl_ss, vl_rs, ol_ss, ol_rs, w_sem,
):
    occ, vir = lax.axis_index("occ"), lax.axis_index("vir")
    ox, oy = occ // 4, occ % 4
    z, core = vir // 2, vir % 2
    i32 = jnp.int32
    barrier = pltpu.get_barrier_semaphore()
    for k in range(1, VIR):
        pl.semaphore_signal(barrier, inc=1, device_id=(occ, (vir + k) % VIR), device_id_type=MESH)
    for k in range(1, OCC):
        pl.semaphore_signal(barrier, inc=1, device_id=((occ + k) % OCC, vir), device_id_type=MESH)

    for part in range(2):
        x_flat[:, part * 6 * TILE : (part + 1) * 6 * TILE] = x_ref[part * FLAT : (part + 1) * FLAT]
    for d in range(6):
        first_row, lane = (d // 2) * TILE, (d % 2) * 3 * TILE
        for start in range(0, TILE, 48):
            row = first_row + start
            shift = (row // FLAT) * 6 * TILE + lane
            y_flat[row % FLAT : row % FLAT + 48, shift : shift + 3 * TILE] = y_ref[d * TILE + start : d * TILE + start + 48]
    pl.semaphore_wait(barrier, VIR + OCC - 2)
    sent = []

    def push(src, dst, ssem, rsem, device):
        copy = pltpu.make_async_remote_copy(src, dst, ssem, rsem, device_id=device, device_id_type=MESH)
        copy.start()
        sent.append(copy)
        return copy

    shards = (x_flat, y_flat)
    landing = (x_got, y_got)
    count = [0, 0]

    def step(rel, axis, k):
        dx, dy = rel // 4, rel % 4
        return ((dx - k) % 4) * 4 + dy if axis == 0 else dx * 4 + (dy - k) % 4

    def target(axis, k):
        return (((ox + k) % 4) * 4 + oy, vir) if axis == 0 else (ox * 4 + (oy + k) % 4, vir)

    def send_sem(array):
        count[array] += 1
        return g_ss.at[array, count[array] - 1]

    def spread(array, axis, rel):
        source = shards[array] if rel == 0 else landing[array].at[rel - 1]
        copies = {}
        for k in (1, 3):
            there = step(rel, axis, k)
            copies[k] = push(
                source, landing[array].at[there - 1], send_sem(array), g_rs.at[array, there - 1, 0], target(axis, k)
            )
        return copies

    def forward(array, axis, rel, copies, flip):
        out = []
        for n, k in enumerate((1, 3)):
            copies[k].wait_recv()
            here = step(rel, axis, k)
            there = step(here, axis, k)
            which = (n + flip) % 2
            rows = pl.ds(*SUBS[which])
            out.append(push(
                landing[array].at[here - 1, rows], landing[array].at[there - 1, rows],
                send_sem(array), g_rs.at[array, there - 1, which], target(axis, k),
            ))
        return out

    first_axis, second_axis = (1, 0), (0, 1)
    first = [spread(array, first_axis[array], 0) for array in range(2)]
    v_labels = [
        push(label_ref.at[k], v_label.at[VIR - k - 1], vl_ss.at[k - 1], vl_rs.at[VIR - k - 1], (occ, (vir + k) % VIR))
        for k in range(1, VIR)
    ]
    second = [{0: spread(array, second_axis[array], 0)} for array in range(2)]
    turned = [[], []]

    def v_pack(q, carry):
        for j in range(8):
            tile = t_ref[index_ref[VPACK + q * 8 + j]]
            v_send[q // 4, q % 4, :, j * TILE : (j + 1) * TILE] = tile
        return carry

    lax.fori_loop(0, VIR * 4, v_pack, 0)

    def rows(h):
        return pl.ds(*CHUNKS[h])

    def v_push(h):
        return [
            push(v_send.at[k, :, rows(h)], v_got.at[VIR - k - 1, :, rows(h)], v_ss.at[h, k - 1], v_rs.at[h, VIR - k - 1],
                 (occ, (vir + k) % VIR))
            for k in range(1, VIR)
        ]

    v_copies = [v_push(h) for h in range(H)]

    middle = [forward(array, first_axis[array], 0, first[array], 0) for array in range(2)]
    for k in (1, 3):
        for array in range(2):
            rel = step(0, first_axis[array], k)
            second[array][rel] = spread(array, second_axis[array], rel)

    line = lax.broadcasted_iota(i32, (VCAP, 128), 0)
    lane = lax.broadcasted_iota(i32, (VCAP, 128), 1)
    places = [jnp.zeros((VCAP, 128), i32)] * 2
    infos = [jnp.zeros((VCAP, 128), i32)] * 2
    for k in range(VIR):
        if k == 0:
            label = label_ref[0]
        else:
            v_labels[VIR - k - 1].wait_recv()
            label = v_label[k - 1]
        for half in range(2):
            hit = (label >= 0) & ((label & 255) == lane + 128 * half)
            places[half] = places[half] + jnp.where(hit, line + k * VCAP, 0)
            infos[half] = infos[half] + jnp.where(hit, (label >> 8) + 1, 0)
    words[...] = jnp.zeros((16, 128), i32)
    for half in range(2):
        words[half : half + 1] = jnp.minimum(jnp.sum(places[half], axis=0, keepdims=True), VIR * VCAP - 1)
        info = jnp.sum(infos[half].astype(jnp.float32), axis=0, keepdims=True)
        column = jnp.transpose(jnp.broadcast_to(info, (128, 128))).astype(i32)
        o_label[half * 8 : half * 8 + 8] = column.reshape(8, 16, 128)
    to_scalar = pltpu.make_async_copy(words.at[0:8], o_index, w_sem.at[0])
    to_scalar.start()
    o_labels = [
        push(o_label.at[k], o_label_got.at[OCC - k - 1], ol_ss.at[k - 1], ol_rs.at[OCC - k - 1], ((occ + k) % OCC, vir))
        for k in range(1, OCC)
    ]
    to_scalar.wait()

    for array in range(2):
        for copy in middle[array]:
            copy.wait_recv()
        rel = step(step(0, first_axis[array], 1), first_axis[array], 1)
        second[array][rel] = spread(array, second_axis[array], rel)
    blocks[BLOCKS] = jnp.zeros((TILE, TILE), jnp.bfloat16)
    for n in range(4):
        for array in range(2):
            rel = list(second[array])[n]
            turned[array] = turned[array] + forward(array, second_axis[array], rel, second[array][rel], n % 2)

    def gather_unpack(array):
        for copy in turned[array]:
            copy.wait_recv()

        def unpack_from(ref, base):
            left, right = ref[:, : 6 * TILE], ref[:, 6 * TILE :]
            strips = (left[:TILE], jnp.concatenate([left[TILE:], right[: 2 * TILE - FLAT]], axis=0), right[2 * TILE - FLAT :])
            for row in range(3):
                for c in range(6):
                    blocks[base + row * 6 + c] = strips[row][:, c * TILE : (c + 1) * TILE]

        unpack_from(shards[array], 0)

        def body(n, carry):
            unpack_from(landing[array].at[n], (n + 1) * 18)
            return carry

        lax.fori_loop(0, OCC - 1, body, 0)

    def cycle_words():
        line16 = lax.broadcasted_iota(i32, (16, 128), 0)
        totals = [jnp.zeros((16, 128), i32)] * 2
        for k in range(OCC):
            if k == 0:
                label = o_label[0]
            else:
                o_labels[OCC - k - 1].wait_recv()
                label = o_label_got[k - 1]
            value = (line16 + k * 16) * 8 + ((label - 1) & 7) + 1
            for half in range(2):
                hit = (label > 0) & (rows_ref[half, 0:1] == k) & (((label - 1) >> 3) == rows_ref[half, 1:2])
                totals[half] = totals[half] + jnp.where(hit, value, 0)
        for half in range(2):
            for j in range(2):
                found = jnp.sum(totals[half][j * 8 : j * 8 + 8], axis=0, keepdims=True)
                block = jnp.where(found > 0, rows_ref[half, 2:3] + 3 * ((found - 1) & 7), BLOCKS)
                tile = jnp.where(found > 0, (found - 1) >> 3, 0)
                words[8 + half * 4 + j : 9 + half * 4 + j] = jnp.clip(block, 0, BLOCKS)
                words[10 + half * 4 + j : 11 + half * 4 + j] = jnp.minimum(tile, 255)
        copy = pltpu.make_async_copy(words.at[8:16], c_index, w_sem.at[1])
        copy.start()
        copy.wait()

    def split(dst, strip, base):
        for j in range(8):
            dst[base + j] = strip[:, j * TILE : (j + 1) * TILE]

    def o_step(h):
        for copy in v_copies[h]:
            copy.wait_recv()
        tiles = small.at[:, pl.ds(0, CHUNKS[h][1])]
        for q in range(4):
            split(tiles, v_send[0, q, rows(h)], q * 8)

        def unpack(q, carry):
            split(tiles, v_got[q // 4, q % 4, rows(h)], (q + 4) * 8)
            return carry

        lax.fori_loop(0, (VIR - 1) * 4, unpack, 0)

        def pack(q, carry):
            for j in range(8):
                o_send[q // 2, q % 2, rows(h), j * TILE : (j + 1) * TILE] = tiles[o_index[q // 16, (q % 16) * 8 + j]]
            return carry

        lax.fori_loop(0, OCC * 2, pack, 0)
        return [
            push(o_send.at[k, :, rows(h)], o_got.at[OCC - k - 1, :, rows(h)], o_ss.at[h, k - 1],
                 o_rs.at[h, OCC - k - 1], ((occ + k) % OCC, vir))
            for k in range(1, OCC)
        ]

    def products(look, tiles, part, held, swap):
        def octet(q, carry):
            owner = q // 3
            for j in range(8):
                row = q * 8 + j
                total = None
                for half in range(2):
                    block = blocks[look(half, row)]
                    tile = tiles[look(2 + half, row)]
                    left, right = (tile, block) if swap else (block, tile)
                    term = jnp.dot(left, right, preferred_element_type=jnp.float32)
                    total = term if total is None else total + term
                part[owner % 2, owner // 2, q % 3, held, j * TILE : (j + 1) * TILE] = total.astype(jnp.bfloat16)
            return carry

        lax.fori_loop(0, ROWS // 8, octet, 0)

    def core_push(n, part, dst, held):
        return push(part.at[1 - core, :, :, held], dst.at[:, :, held], core_ss.at[n], core_rs.at[n], (occ, z * 2 + 1 - core))

    def z_push(n, copy, part, dst, z_got, held):
        copy.wait_recv()

        def add(q, carry):
            total = part[core, q // 3, q % 3, held].astype(jnp.float32) + dst[q // 3, q % 3, held].astype(jnp.float32)
            dst[q // 3, q % 3, held] = total.astype(jnp.bfloat16)
            return carry

        lax.fori_loop(0, 12, add, 0)
        return [
            push(dst.at[(z + k) % 4, :, held], z_got.at[4 - k - 1, :, held], z_ss.at[n, k - 1], z_rs.at[n, 4 - k - 1],
                 (occ, ((z + k) % 4) * 2 + core))
            for k in (1, 3, 2)
        ]

    def finish(copies, dst, z_got, out, held):
        for copy in copies:
            copy.wait_recv()
        for i in range(3):
            total = dst[z, i, held].astype(jnp.float32)
            for k in range(3):
                total = total + z_got[k, i, held].astype(jnp.float32)
            for j in range(8):
                out[i * 8 + j, held] = total[:, j * TILE : (j + 1) * TILE]

    whole = pl.ds(0, TILE)
    o_copies = [o_step(h) for h in range(H)]
    gather_unpack(0)
    products(lambda n, row: index_ref[LADDER + n * ROWS + row], t_ref, l_part, whole, False)
    l_copy = core_push(H, l_part, l_core, whole)
    cycle_words()
    gather_unpack(1)
    l_copies = z_push(H, l_copy, l_part, l_core, l_z, whole)
    c_copies = []
    for h in range(H):
        for copy in o_copies[h]:
            copy.wait_recv()
        tiles = small.at[:, pl.ds(0, CHUNKS[h][1])]
        for j in range(2):
            split(tiles, o_send[0, j, rows(h)], j * 8)

        def unpack(q, carry):
            split(tiles, o_got[q // 2, q % 2, rows(h)], (q + 2) * 8)
            return carry

        lax.fori_loop(0, (OCC - 1) * 2, unpack, 0)
        products(lambda n, row: c_index[(row // 128) * 4 + n, row % 128], tiles, c_part, rows(h), True)
        c_copies.append(core_push(h, c_part, c_core, rows(h)))
        if h > 0:
            c_copies[h - 1] = z_push(h - 1, c_copies[h - 1], c_part, c_core, c_z, rows(h - 1))
    finish(l_copies, l_core, l_z, ladder_ref, whole)
    c_copies[H - 1] = z_push(H - 1, c_copies[H - 1], c_part, c_core, c_z, rows(H - 1))
    for h in range(H):
        finish(c_copies[h], c_core, c_z, cycle_ref, rows(h))
    for copy in sent:
        copy.wait_send()


def main_call(index, labels, rows, tiles, x, y):
    bf16 = jnp.bfloat16
    vmem = pl.BlockSpec(memory_space=pltpu.VMEM)
    dma = pltpu.SemaphoreType.DMA
    out = jax.ShapeDtypeStruct((24, TILE, TILE), jnp.float32)
    return pl.pallas_call(
        main_kernel,
        out_shape=(out, out),
        in_specs=[pl.BlockSpec(memory_space=pltpu.SMEM)] + [vmem] * 5,
        out_specs=(vmem, vmem),
        scratch_shapes=[
            pltpu.VMEM((FLAT, 12 * TILE), bf16),
            pltpu.VMEM((FLAT, 12 * TILE), bf16),
            pltpu.VMEM((OCC - 1, FLAT, 12 * TILE), bf16),
            pltpu.VMEM((OCC - 1, FLAT, 12 * TILE), bf16),
            pltpu.VMEM((BLOCKS + 1, TILE, TILE), bf16),
            pltpu.VMEM((VIR, 4, TILE, WIDE), bf16),
            pltpu.VMEM((VIR - 1, 4, TILE, WIDE), bf16),
            pltpu.VMEM((OCC, 2, TILE, WIDE), bf16),
            pltpu.VMEM((OCC - 1, 2, TILE, WIDE), bf16),
            pltpu.VMEM((256, MOST, TILE), bf16),
            pltpu.VMEM((2, 4, 3, TILE, WIDE), bf16),
            pltpu.VMEM((4, 3, TILE, WIDE), bf16),
            pltpu.VMEM((3, 3, TILE, WIDE), bf16),
            pltpu.VMEM((2, 4, 3, TILE, WIDE), bf16),
            pltpu.VMEM((4, 3, TILE, WIDE), bf16),
            pltpu.VMEM((3, 3, TILE, WIDE), bf16),
            pltpu.VMEM((VIR - 1, VCAP, 128), jnp.int32),
            pltpu.VMEM((OCC, 16, 128), jnp.int32),
            pltpu.VMEM((OCC - 1, 16, 128), jnp.int32),
            pltpu.VMEM((16, 128), jnp.int32),
            pltpu.SMEM((8, 128), jnp.int32),
            pltpu.SMEM((8, 128), jnp.int32),
            dma((2, 20)), dma((2, OCC - 1, 2)),
            dma((H, VIR - 1)), dma((H, VIR - 1)),
            dma((H, OCC - 1)), dma((H, OCC - 1)),
            dma((H + 1,)), dma((H + 1,)),
            dma((H + 1, 3)), dma((H + 1, 3)),
            dma((VIR - 1,)), dma((VIR - 1,)), dma((OCC - 1,)), dma((OCC - 1,)), dma((2,)),
        ],
        compiler_params=pltpu.CompilerParams(
            collective_id=1, has_side_effects=True, vmem_limit_bytes=63_000_000
        ),
        cost_estimate=pl.CostEstimate(flops=8 * ROWS * TILE**3, bytes_accessed=14_000_000, transcendentals=0),
        name="contract",
    )(index, labels, rows, tiles, x, y)


def on_device(t_tiles, t_index, cycle_map, ladder_slots, cycle_slots, x_ints, y_ints):
    occ = lax.axis_index("occ")
    vir = lax.axis_index("vir")
    i32 = jnp.int32
    pair_range = jnp.arange(2, dtype=i32)
    local = t_index[:, 0] - occ * PAIRS
    first = t_index[:, 1]
    second = t_index[:, 2]
    group = second // VT

    strip = local * NV + first
    same = strip[:, None] == strip[None, :]
    smaller = same & (second[None, :] < first[:, None])
    here = same & (group[None, :] == vir)
    rank_all = jnp.sum(smaller.astype(i32), axis=1)
    which = jnp.sum((smaller & here).astype(i32), axis=1)
    own_count = jnp.sum(here.astype(i32), axis=1)
    together = group[:, None] == group[None, :]
    rank_second = jnp.sum((same & together & (second[None, :] < second[:, None])).astype(i32), axis=1)
    start = jnp.sum((together & (local[None, :] < local[:, None])).astype(i32), axis=1)

    position = ((group - vir) % VIR) * VCAP + start + rank_second * own_count + which
    own_map = lax.dynamic_slice_in_dim(cycle_map, occ * PAIRS, PAIRS, 0)
    to_group = jnp.sum(
        jnp.where(local[:, None] == jnp.arange(PAIRS, dtype=i32)[None, :], (own_map[None, :] - occ) % OCC, 0), axis=1
    )
    target = to_group * 16 + rank_second * 8 + rank_all
    label = target + 256 * (first * 8 + second % VT)
    pick = jnp.arange(VIR * VCAP, dtype=i32)[:, None] == position[None, :]
    packed_pick = jnp.sum(jnp.where(pick, label * 128 + jnp.arange(128, dtype=i32) + 1, 0), axis=1)
    v_pack = jnp.where(packed_pick > 0, (packed_pick - 1) % 128, 0)
    labels = jnp.where(packed_pick > 0, (packed_pick - 1) // 128, -1)
    labels = jnp.broadcast_to(labels.reshape(VIR, VCAP, 1), (VIR, VCAP, 128))

    def ahead(group):
        return ((group // 4 - occ // 4) % 4) * 4 + (group % 4 - occ % 4) % 4

    tile_key = (local * 2 + which) * NV + second
    row_key = (ladder_slots[:, 0][None, :] * 2 + pair_range[:, None]) * NV + ladder_slots[:, 2][None, :]
    match = row_key[:, :, None] == tile_key[None, None, :]
    packed = jnp.arange(128, dtype=i32) * 8 + first - vir * VT + 1
    found = jnp.sum(jnp.where(match, packed, 0), axis=-1)
    ladder_tile = jnp.where(found > 0, (found - 1) // 8, 0)
    x_row = ladder_slots[:, 1]
    x_block = (ahead(x_row // 3) * 3 + x_row % 3) * VT
    ladder_block = jnp.where(found > 0, x_block[None, :] + (found - 1) % 8, BLOCKS)

    s, a, b = cycle_slots[:, 0], cycle_slots[:, 1], cycle_slots[:, 2]
    pairs = jnp.arange(OCC * PAIRS, dtype=i32)
    owned = (cycle_map[None, :] == occ) & (pairs[None, :] % PAIRS == s[:, None])
    ahead_of = jnp.sum(jnp.where(owned, (pairs // PAIRS - occ) % OCC, 0), axis=1)
    rows = jnp.stack([ahead_of, a, ahead(b // 3) * 18 + b % 3], axis=0)
    rows = jnp.pad(rows, ((0, 5), (0, 256 - ROWS)), constant_values=-1).reshape(8, 2, 128).transpose(1, 0, 2)

    index = jnp.concatenate([v_pack, ladder_block.reshape(-1), ladder_tile.reshape(-1)])
    ladder, cycle = main_call(index, labels, rows, t_tiles.reshape(128, TILE, TILE), x_ints, y_ints)
    return ladder.reshape(24, AREA), cycle.reshape(24, AREA)


def solution(mesh):
    return jax.shard_map(
        on_device,
        mesh=mesh,
        in_specs=(
            P(("occ", "vir"), None),
            P(("occ", "vir"), None),
            P(),
            P("occ", None),
            P("occ", None),
            P("occ", "vir"),
            P("vir", "occ"),
        ),
        out_specs=(P(("occ", "vir"), None), P(("occ", "vir"), None)),
        check_vma=False,
    )
```

```python
import functools

import jax
import jax.numpy as jnp
from jax import lax
from jax.experimental import pallas as pl
from jax.experimental.pallas import tpu as pltpu
from jax.sharding import PartitionSpec as P

TILE = 96
NV = 48
AREA = TILE * TILE
OCC = 16
VIR = 8
VT = 6
PAIRS = 16
VCAP = 32
BLOCKS = 288
ROWS = 192
WIDE = 8 * TILE
CHUNKS = ((0, 32), (32, 32), (64, 32))
H = len(CHUNKS)
MOST = max(n for _, n in CHUNKS)
FLAT = 144
SUBS = ((0, 80), (80, 64))
MESH = pl.DeviceIdType.MESH
VPACK, LADDER = 0, 256


def main_kernel(
    index_ref, label_ref, rows_ref, t_ref, x_ref, y_ref, ladder_ref, cycle_ref,
    x_flat, y_flat, x_got, y_got, blocks, v_send, v_got, o_send, o_got, small,
    l_part, l_core, l_z, c_part, c_core, c_z,
    v_label, o_label, o_label_got, words, o_index, c_index,
    g_ss, g_rs, v_ss, v_rs, o_ss, o_rs, core_ss, core_rs, z_ss, z_rs,
    vl_ss, vl_rs, ol_ss, ol_rs, w_sem,
):
    occ, vir = lax.axis_index("occ"), lax.axis_index("vir")
    ox, oy = occ // 4, occ % 4
    z, core = vir // 2, vir % 2
    i32 = jnp.int32
    barrier = pltpu.get_barrier_semaphore()
    for k in range(1, VIR):
        pl.semaphore_signal(barrier, inc=1, device_id=(occ, (vir + k) % VIR), device_id_type=MESH)
    for k in range(1, OCC):
        pl.semaphore_signal(barrier, inc=1, device_id=((occ + k) % OCC, vir), device_id_type=MESH)

    for part in range(2):
        x_flat[:, part * 6 * TILE : (part + 1) * 6 * TILE] = x_ref[part * FLAT : (part + 1) * FLAT]
    for d in range(6):
        first_row, lane = (d // 2) * TILE, (d % 2) * 3 * TILE
        strip = jnp.transpose(y_ref[:, d * TILE : (d + 1) * TILE])
        for start in range(0, TILE, 48):
            row = first_row + start
            shift = (row // FLAT) * 6 * TILE + lane
            y_flat[row % FLAT : row % FLAT + 48, shift : shift + 3 * TILE] = strip[start : start + 48]
    pl.semaphore_wait(barrier, VIR + OCC - 2)
    sent = []

    def push(src, dst, ssem, rsem, device):
        copy = pltpu.make_async_remote_copy(src, dst, ssem, rsem, device_id=device, device_id_type=MESH)
        copy.start()
        sent.append(copy)
        return copy

    shards = (x_flat, y_flat)
    landing = (x_got, y_got)
    count = [0, 0]

    def step(rel, axis, k):
        dx, dy = rel // 4, rel % 4
        return ((dx - k) % 4) * 4 + dy if axis == 0 else dx * 4 + (dy - k) % 4

    def target(axis, k):
        return (((ox + k) % 4) * 4 + oy, vir) if axis == 0 else (ox * 4 + (oy + k) % 4, vir)

    def send_sem(array):
        count[array] += 1
        return g_ss.at[array, count[array] - 1]

    def spread(array, axis, rel):
        source = shards[array] if rel == 0 else landing[array].at[rel - 1]
        copies = {}
        for k in (1, 3):
            there = step(rel, axis, k)
            copies[k] = push(
                source, landing[array].at[there - 1], send_sem(array), g_rs.at[array, there - 1, 0], target(axis, k)
            )
        return copies

    def forward(array, axis, rel, copies, flip):
        out = []
        for n, k in enumerate((1, 3)):
            copies[k].wait_recv()
            here = step(rel, axis, k)
            there = step(here, axis, k)
            which = (n + flip) % 2
            rows = pl.ds(*SUBS[which])
            out.append(push(
                landing[array].at[here - 1, rows], landing[array].at[there - 1, rows],
                send_sem(array), g_rs.at[array, there - 1, which], target(axis, k),
            ))
        return out

    first_axis, second_axis = (1, 0), (0, 1)
    first = [spread(array, first_axis[array], 0) for array in range(2)]
    v_labels = [
        push(label_ref.at[k], v_label.at[VIR - k - 1], vl_ss.at[k - 1], vl_rs.at[VIR - k - 1], (occ, (vir + k) % VIR))
        for k in range(1, VIR)
    ]
    second = [{0: spread(array, second_axis[array], 0)} for array in range(2)]
    turned = [[], []]

    def v_pack(q, carry):
        for j in range(8):
            tile = t_ref[index_ref[VPACK + q * 8 + j]]
            v_send[q // 4, q % 4, :, j * TILE : (j + 1) * TILE] = tile
        return carry

    lax.fori_loop(0, VIR * 4, v_pack, 0)

    def rows(h):
        return pl.ds(*CHUNKS[h])

    def v_push(h):
        return [
            push(v_send.at[k, :, rows(h)], v_got.at[VIR - k - 1, :, rows(h)], v_ss.at[h, k - 1], v_rs.at[h, VIR - k - 1],
                 (occ, (vir + k) % VIR))
            for k in range(1, VIR)
        ]

    v_copies = [v_push(h) for h in range(H)]

    middle = [forward(array, first_axis[array], 0, first[array], 0) for array in range(2)]
    for k in (1, 3):
        for array in range(2):
            rel = step(0, first_axis[array], k)
            second[array][rel] = spread(array, second_axis[array], rel)

    line = lax.broadcasted_iota(i32, (VCAP, 128), 0)
    lane = lax.broadcasted_iota(i32, (VCAP, 128), 1)
    places = [jnp.zeros((VCAP, 128), i32)] * 2
    infos = [jnp.zeros((VCAP, 128), i32)] * 2
    for k in range(VIR):
        if k == 0:
            label = label_ref[0]
        else:
            v_labels[VIR - k - 1].wait_recv()
            label = v_label[k - 1]
        for half in range(2):
            hit = (label >= 0) & ((label & 255) == lane + 128 * half)
            places[half] = places[half] + jnp.where(hit, line + k * VCAP, 0)
            infos[half] = infos[half] + jnp.where(hit, (label >> 8) + 1, 0)
    words[...] = jnp.zeros((16, 128), i32)
    for half in range(2):
        words[half : half + 1] = jnp.minimum(jnp.sum(places[half], axis=0, keepdims=True), VIR * VCAP - 1)
        info = jnp.sum(infos[half].astype(jnp.float32), axis=0, keepdims=True)
        column = jnp.transpose(jnp.broadcast_to(info, (128, 128))).astype(i32)
        o_label[half * 8 : half * 8 + 8] = column.reshape(8, 16, 128)
    to_scalar = pltpu.make_async_copy(words.at[0:8], o_index, w_sem.at[0])
    to_scalar.start()
    o_labels = [
        push(o_label.at[k], o_label_got.at[OCC - k - 1], ol_ss.at[k - 1], ol_rs.at[OCC - k - 1], ((occ + k) % OCC, vir))
        for k in range(1, OCC)
    ]
    to_scalar.wait()

    for array in range(2):
        for copy in middle[array]:
            copy.wait_recv()
        rel = step(step(0, first_axis[array], 1), first_axis[array], 1)
        second[array][rel] = spread(array, second_axis[array], rel)
    blocks[BLOCKS] = jnp.zeros((TILE, TILE), jnp.bfloat16)
    for n in range(4):
        for array in range(2):
            rel = list(second[array])[n]
            turned[array] = turned[array] + forward(array, second_axis[array], rel, second[array][rel], n % 2)

    def gather_unpack(array):
        for copy in turned[array]:
            copy.wait_recv()

        def unpack_from(ref, base):
            left, right = ref[:, : 6 * TILE], ref[:, 6 * TILE :]
            strips = (left[:TILE], jnp.concatenate([left[TILE:], right[: 2 * TILE - FLAT]], axis=0), right[2 * TILE - FLAT :])
            for row in range(3):
                for c in range(6):
                    blocks[base + row * 6 + c] = strips[row][:, c * TILE : (c + 1) * TILE]

        unpack_from(shards[array], 0)

        def body(n, carry):
            unpack_from(landing[array].at[n], (n + 1) * 18)
            return carry

        lax.fori_loop(0, OCC - 1, body, 0)

    def cycle_words():
        line16 = lax.broadcasted_iota(i32, (16, 128), 0)
        totals = [jnp.zeros((16, 128), i32)] * 2
        for k in range(OCC):
            if k == 0:
                label = o_label[0]
            else:
                o_labels[OCC - k - 1].wait_recv()
                label = o_label_got[k - 1]
            value = (line16 + k * 16) * 8 + ((label - 1) & 7) + 1
            for half in range(2):
                hit = (label > 0) & (rows_ref[half, 0:1] == k) & (((label - 1) >> 3) == rows_ref[half, 1:2])
                totals[half] = totals[half] + jnp.where(hit, value, 0)
        for half in range(2):
            for j in range(2):
                found = jnp.sum(totals[half][j * 8 : j * 8 + 8], axis=0, keepdims=True)
                block = jnp.where(found > 0, rows_ref[half, 2:3] + 3 * ((found - 1) & 7), BLOCKS)
                tile = jnp.where(found > 0, (found - 1) >> 3, 0)
                words[8 + half * 4 + j : 9 + half * 4 + j] = jnp.clip(block, 0, BLOCKS)
                words[10 + half * 4 + j : 11 + half * 4 + j] = jnp.minimum(tile, 255)
        copy = pltpu.make_async_copy(words.at[8:16], c_index, w_sem.at[1])
        copy.start()
        copy.wait()

    def split(dst, strip, base):
        for j in range(8):
            dst[base + j] = strip[:, j * TILE : (j + 1) * TILE]

    def o_step(h):
        for copy in v_copies[h]:
            copy.wait_recv()
        tiles = small.at[:, pl.ds(0, CHUNKS[h][1])]
        for q in range(4):
            split(tiles, v_send[0, q, rows(h)], q * 8)

        def unpack(q, carry):
            split(tiles, v_got[q // 4, q % 4, rows(h)], (q + 4) * 8)
            return carry

        lax.fori_loop(0, (VIR - 1) * 4, unpack, 0)

        def pack(q, carry):
            for j in range(8):
                o_send[q // 2, q % 2, rows(h), j * TILE : (j + 1) * TILE] = tiles[o_index[q // 16, (q % 16) * 8 + j]]
            return carry

        lax.fori_loop(0, OCC * 2, pack, 0)
        return [
            push(o_send.at[k, :, rows(h)], o_got.at[OCC - k - 1, :, rows(h)], o_ss.at[h, k - 1],
                 o_rs.at[h, OCC - k - 1], ((occ + k) % OCC, vir))
            for k in range(1, OCC)
        ]

    def products(look, tiles, part, held, swap, dest):
        def octet(n, carry):
            side, i = n // 3, n % 3
            for j in range(8):
                row = ((dest * 2 + side) * 3 + i) * 8 + j
                total = None
                for half in range(2):
                    block = blocks[look(half, row)]
                    tile = tiles[look(2 + half, row)]
                    left, right = (tile, block) if swap else (block, tile)
                    term = jnp.dot(left, right, preferred_element_type=jnp.float32)
                    total = term if total is None else total + term
                part[side, dest, i, held, j * TILE : (j + 1) * TILE] = total.astype(jnp.bfloat16)
            return carry

        lax.fori_loop(0, 6, octet, 0)

    def core_push(n, k, part, dst, held):
        dest = (z + k) % 4
        return push(
            part.at[1 - core, dest, :, held], dst.at[dest, :, held],
            core_ss.at[n, k], core_rs.at[n, k], (occ, z * 2 + 1 - core),
        )

    def z_push(n, k, copy, part, dst, z_got, held):
        copy.wait_recv()
        dest = (z + k) % 4
        for i in range(3):
            total = part[core, dest, i, held].astype(jnp.float32) + dst[dest, i, held].astype(jnp.float32)
            dst[dest, i, held] = total.astype(jnp.bfloat16)
        if k == 0:
            return []
        return [push(
            dst.at[dest, :, held], z_got.at[4 - k - 1, :, held], z_ss.at[n, k - 1], z_rs.at[n, 4 - k - 1],
            (occ, dest * 2 + core),
        )]

    def all_rows(n, look, tiles, part, dst, z_got, held, swap):
        copies, before = [], None
        for k in (2, 1, 3, 0):
            products(look, tiles, part, held, swap, (z + k) % 4)
            copy = core_push(n, k, part, dst, held)
            if before is not None:
                copies = copies + z_push(n, before[0], before[1], part, dst, z_got, held)
            before = (k, copy)
        return copies, before

    def finish(copies, dst, z_got, out, held):
        for copy in copies:
            copy.wait_recv()
        for i in range(3):
            total = dst[z, i, held].astype(jnp.float32)
            for k in range(3):
                total = total + z_got[k, i, held].astype(jnp.float32)
            for j in range(8):
                out[i * 8 + j, held] = total[:, j * TILE : (j + 1) * TILE]

    whole = pl.ds(0, TILE)
    o_copies = [o_step(h) for h in range(H)]
    gather_unpack(0)
    l_copies, rest = all_rows(
        H, lambda n, row: index_ref[LADDER + n * ROWS + row], t_ref, l_part, l_core, l_z, whole, False
    )
    cycle_words()
    gather_unpack(1)
    l_copies = l_copies + z_push(H, *rest, l_part, l_core, l_z, whole)
    c_copies, rests = [], []
    for h in range(H):
        for copy in o_copies[h]:
            copy.wait_recv()
        tiles = small.at[:, pl.ds(0, CHUNKS[h][1])]
        for j in range(2):
            split(tiles, o_send[0, j, rows(h)], j * 8)

        def unpack(q, carry):
            split(tiles, o_got[q // 2, q % 2, rows(h)], (q + 2) * 8)
            return carry

        lax.fori_loop(0, (OCC - 1) * 2, unpack, 0)
        copies, rest = all_rows(
            h, lambda n, row: c_index[(row // 128) * 4 + n, row % 128], tiles, c_part, c_core, c_z, rows(h), True
        )
        c_copies.append(copies)
        rests.append(rest)
    finish(l_copies, l_core, l_z, ladder_ref, whole)
    for h in range(H):
        z_push(h, *rests[h], c_part, c_core, c_z, rows(h))
        finish(c_copies[h], c_core, c_z, cycle_ref, rows(h))
    for copy in sent:
        copy.wait_send()


def main_call(index, labels, rows, tiles, x, y):
    bf16 = jnp.bfloat16
    vmem = pl.BlockSpec(memory_space=pltpu.VMEM)
    dma = pltpu.SemaphoreType.DMA
    out = jax.ShapeDtypeStruct((24, TILE, TILE), jnp.float32)
    return pl.pallas_call(
        main_kernel,
        out_shape=(out, out),
        in_specs=[pl.BlockSpec(memory_space=pltpu.SMEM)] + [vmem] * 5,
        out_specs=(vmem, vmem),
        scratch_shapes=[
            pltpu.VMEM((FLAT, 12 * TILE), bf16),
            pltpu.VMEM((FLAT, 12 * TILE), bf16),
            pltpu.VMEM((OCC - 1, FLAT, 12 * TILE), bf16),
            pltpu.VMEM((OCC - 1, FLAT, 12 * TILE), bf16),
            pltpu.VMEM((BLOCKS + 1, TILE, TILE), bf16),
            pltpu.VMEM((VIR, 4, TILE, WIDE), bf16),
            pltpu.VMEM((VIR - 1, 4, TILE, WIDE), bf16),
            pltpu.VMEM((OCC, 2, TILE, WIDE), bf16),
            pltpu.VMEM((OCC - 1, 2, TILE, WIDE), bf16),
            pltpu.VMEM((256, MOST, TILE), bf16),
            pltpu.VMEM((2, 4, 3, TILE, WIDE), bf16),
            pltpu.VMEM((4, 3, TILE, WIDE), bf16),
            pltpu.VMEM((3, 3, TILE, WIDE), bf16),
            pltpu.VMEM((2, 4, 3, TILE, WIDE), bf16),
            pltpu.VMEM((4, 3, TILE, WIDE), bf16),
            pltpu.VMEM((3, 3, TILE, WIDE), bf16),
            pltpu.VMEM((VIR - 1, VCAP, 128), jnp.int32),
            pltpu.VMEM((OCC, 16, 128), jnp.int32),
            pltpu.VMEM((OCC - 1, 16, 128), jnp.int32),
            pltpu.VMEM((16, 128), jnp.int32),
            pltpu.SMEM((8, 128), jnp.int32),
            pltpu.SMEM((8, 128), jnp.int32),
            dma((2, 20)), dma((2, OCC - 1, 2)),
            dma((H, VIR - 1)), dma((H, VIR - 1)),
            dma((H, OCC - 1)), dma((H, OCC - 1)),
            dma((H + 1, 4)), dma((H + 1, 4)),
            dma((H + 1, 3)), dma((H + 1, 3)),
            dma((VIR - 1,)), dma((VIR - 1,)), dma((OCC - 1,)), dma((OCC - 1,)), dma((2,)),
        ],
        compiler_params=pltpu.CompilerParams(
            collective_id=1, has_side_effects=True, vmem_limit_bytes=63_000_000
        ),
        cost_estimate=pl.CostEstimate(flops=8 * ROWS * TILE**3, bytes_accessed=14_000_000, transcendentals=0),
        name="contract",
    )(index, labels, rows, tiles, x, y)


def on_device(t_tiles, t_index, cycle_map, ladder_slots, cycle_slots, x_ints, y_ints):
    occ = lax.axis_index("occ")
    vir = lax.axis_index("vir")
    i32 = jnp.int32
    pair_range = jnp.arange(2, dtype=i32)
    local = t_index[:, 0] - occ * PAIRS
    first = t_index[:, 1]
    second = t_index[:, 2]
    group = second // VT

    strip = local * NV + first
    same = strip[:, None] == strip[None, :]
    smaller = same & (second[None, :] < first[:, None])
    here = same & (group[None, :] == vir)
    rank_all = jnp.sum(smaller.astype(i32), axis=1)
    which = jnp.sum((smaller & here).astype(i32), axis=1)
    own_count = jnp.sum(here.astype(i32), axis=1)
    together = group[:, None] == group[None, :]
    rank_second = jnp.sum((same & together & (second[None, :] < second[:, None])).astype(i32), axis=1)
    start = jnp.sum((together & (local[None, :] < local[:, None])).astype(i32), axis=1)

    position = ((group - vir) % VIR) * VCAP + start + rank_second * own_count + which
    own_map = lax.dynamic_slice_in_dim(cycle_map, occ * PAIRS, PAIRS, 0)
    to_group = jnp.sum(
        jnp.where(local[:, None] == jnp.arange(PAIRS, dtype=i32)[None, :], (own_map[None, :] - occ) % OCC, 0), axis=1
    )
    target = to_group * 16 + rank_second * 8 + rank_all
    label = target + 256 * (first * 8 + second % VT)
    pick = jnp.arange(VIR * VCAP, dtype=i32)[:, None] == position[None, :]
    packed_pick = jnp.sum(jnp.where(pick, label * 128 + jnp.arange(128, dtype=i32) + 1, 0), axis=1)
    v_pack = jnp.where(packed_pick > 0, (packed_pick - 1) % 128, 0)
    labels = jnp.where(packed_pick > 0, (packed_pick - 1) // 128, -1)
    labels = jnp.broadcast_to(labels.reshape(VIR, VCAP, 1), (VIR, VCAP, 128))

    def ahead(group):
        return ((group // 4 - occ // 4) % 4) * 4 + (group % 4 - occ % 4) % 4

    tile_key = (local * 2 + which) * NV + second
    row_key = (ladder_slots[:, 0][None, :] * 2 + pair_range[:, None]) * NV + ladder_slots[:, 2][None, :]
    match = row_key[:, :, None] == tile_key[None, None, :]
    packed = jnp.arange(128, dtype=i32) * 8 + first - vir * VT + 1
    found = jnp.sum(jnp.where(match, packed, 0), axis=-1)
    ladder_tile = jnp.where(found > 0, (found - 1) // 8, 0)
    x_row = ladder_slots[:, 1]
    x_block = (ahead(x_row // 3) * 3 + x_row % 3) * VT
    ladder_block = jnp.where(found > 0, x_block[None, :] + (found - 1) % 8, BLOCKS)

    s, a, b = cycle_slots[:, 0], cycle_slots[:, 1], cycle_slots[:, 2]
    pairs = jnp.arange(OCC * PAIRS, dtype=i32)
    owned = (cycle_map[None, :] == occ) & (pairs[None, :] % PAIRS == s[:, None])
    ahead_of = jnp.sum(jnp.where(owned, (pairs // PAIRS - occ) % OCC, 0), axis=1)
    rows = jnp.stack([ahead_of, a, ahead(b // 3) * 18 + b % 3], axis=0)
    rows = jnp.pad(rows, ((0, 5), (0, 256 - ROWS)), constant_values=-1).reshape(8, 2, 128).transpose(1, 0, 2)

    index = jnp.concatenate([v_pack, ladder_block.reshape(-1), ladder_tile.reshape(-1)])
    ladder, cycle = main_call(index, labels, rows, t_tiles.reshape(128, TILE, TILE), x_ints, y_ints.T)
    return ladder.reshape(24, AREA), cycle.reshape(24, AREA)


def solution(mesh):
    return jax.shard_map(
        on_device,
        mesh=mesh,
        in_specs=(
            P(("occ", "vir"), None),
            P(("occ", "vir"), None),
            P(),
            P("occ", None),
            P("occ", None),
            P("occ", "vir"),
            P("vir", "occ"),
        ),
        out_specs=(P(("occ", "vir"), None), P(("occ", "vir"), None)),
        check_vma=False,
    )
```

```python
import functools

import jax
import jax.numpy as jnp
from jax import lax
from jax.experimental import pallas as pl
from jax.experimental.pallas import tpu as pltpu
from jax.sharding import PartitionSpec as P

TILE = 96
NV = 48
AREA = TILE * TILE
OCC = 16
VIR = 8
VT = 6
PAIRS = 16
VCAP = 32
BLOCKS = 288
ROWS = 192
WIDE = 8 * TILE
CHUNKS = ((0, 32), (32, 32), (64, 32))
H = len(CHUNKS)
MOST = max(n for _, n in CHUNKS)
FLAT = 144
SUBS = ((0, 80), (80, 64))
MESH = pl.DeviceIdType.MESH


def main_kernel(
    list_ref, map_ref, rows_ref, t_ref, x_ref, y_ref, ladder_ref, cycle_ref,
    index_ref, label_ref, first_words,
    x_flat, y_flat, x_got, y_got, blocks, v_send, v_got, o_send, o_got, small,
    l_part, l_core, l_z, c_part, c_core, c_z,
    v_label, o_label, o_label_got, words, o_index, c_index,
    g_ss, g_rs, v_ss, v_rs, o_ss, o_rs, core_ss, core_rs, z_ss, z_rs,
    vl_ss, vl_rs, ol_ss, ol_rs, w_sem,
):
    occ, vir = lax.axis_index("occ"), lax.axis_index("vir")
    ox, oy = occ // 4, occ % 4
    z, core = vir // 2, vir % 2
    i32 = jnp.int32
    barrier = pltpu.get_barrier_semaphore()
    for k in range(1, VIR):
        pl.semaphore_signal(barrier, inc=1, device_id=(occ, (vir + k) % VIR), device_id_type=MESH)
    for k in range(1, OCC):
        pl.semaphore_signal(barrier, inc=1, device_id=((occ + k) % OCC, vir), device_id_type=MESH)

    for part in range(2):
        x_flat[:, part * 6 * TILE : (part + 1) * 6 * TILE] = x_ref[part * FLAT : (part + 1) * FLAT]
    for d in range(6):
        first_row, lane = (d // 2) * TILE, (d % 2) * 3 * TILE
        strip = jnp.transpose(y_ref[:, d * TILE : (d + 1) * TILE])
        for start in range(0, TILE, 48):
            row = first_row + start
            shift = (row // FLAT) * 6 * TILE + lane
            y_flat[row % FLAT : row % FLAT + 48, shift : shift + 3 * TILE] = strip[start : start + 48]
    pl.semaphore_wait(barrier, VIR + OCC - 2)
    sent = []

    def push(src, dst, ssem, rsem, device):
        copy = pltpu.make_async_remote_copy(src, dst, ssem, rsem, device_id=device, device_id_type=MESH)
        copy.start()
        sent.append(copy)
        return copy

    def column(row):
        return jnp.transpose(jnp.broadcast_to(row.astype(jnp.float32), (128, 128))).astype(i32)

    def total(mask, value=1):
        return jnp.sum(jnp.where(mask, value, 0), axis=0, keepdims=True)

    def tile_words():
        lane = lax.broadcasted_iota(i32, (128, 128), 1)
        at = [jnp.broadcast_to(list_ref[:, n : n + 1], (128, 128)) for n in range(3)]
        local, first, second = at[0] - occ * PAIRS, at[1], at[2]
        group = (second * 43) >> 8
        k_local, k_first, k_second = (jnp.transpose(v.astype(jnp.float32)).astype(i32) for v in (local, first, second))
        k_group = (k_second * 43) >> 8
        same = (local == k_local) & (first == k_first)
        smaller = same & (second < k_first)
        here = same & (group == vir)
        together = group == k_group
        rank_all, which, own_count = total(smaller), total(smaller & here), total(here)
        rank_second = total(same & together & (second < k_second))
        start = total(together & (local < k_local))
        k_local, k_first, k_second, k_group = (v[0:1] for v in (k_local, k_first, k_second, k_group))

        position = ((k_group - vir) & 7) * VCAP + start + rank_second * own_count + which
        one = lax.broadcasted_iota(i32, (PAIRS, OCC), 1) == occ
        ahead = (jnp.sum(jnp.where(one, map_ref[...], 0), axis=1, keepdims=True) - occ) & 15
        to_group = total(lax.broadcasted_iota(i32, (PAIRS, 128), 0) == k_local, jnp.broadcast_to(ahead, (PAIRS, 128)))
        label = to_group * 16 + rank_second * 8 + rank_all + 256 * (k_first * 8 + k_second - 6 * k_group)
        places = column(position)
        values = column(label * 128 + lane[0:1] + 1)
        first_words[...] = jnp.zeros((16, 128), i32)
        for half in range(2):
            found = total(places == lane + 128 * half, values)
            first_words[half : half + 1] = jnp.where(found > 0, (found - 1) & 127, 0)
            went = column(jnp.where(found > 0, (found - 1) >> 7, -1))
            label_ref[half * 4 : half * 4 + 4] = went.reshape(4, VCAP, 128)

        keys = column((k_local * 2 + which) * NV + k_second)
        values = column(lane[0:1] * 8 + k_first - vir * VT + 1)
        for half in range(2):
            s, a, b = (rows_ref[half, n : n + 1] for n in (3, 4, 5))
            third = (a * 171) >> 9
            base = (ring_ahead(third) * 3 + a - 3 * third) * VT
            for j in range(2):
                found = total(keys == (s * 2 + j) * NV + b, values)
                block = jnp.where(found > 0, base + ((found - 1) & 7), BLOCKS)
                tile = jnp.where(found > 0, (found - 1) >> 3, 0)
                first_words[2 + half * 4 + j : 3 + half * 4 + j] = jnp.clip(block, 0, BLOCKS)
                first_words[4 + half * 4 + j : 5 + half * 4 + j] = jnp.clip(tile, 0, 127)
        copy = pltpu.make_async_copy(first_words, index_ref, w_sem.at[2])
        copy.start()
        copy.wait()

    def ring_ahead(group):
        return (((group >> 2) - ox) & 3) * 4 + (((group & 3) - oy) & 3)

    shards = (x_flat, y_flat)
    landing = (x_got, y_got)
    count = [0, 0]

    def step(rel, axis, k):
        dx, dy = rel // 4, rel % 4
        return ((dx - k) % 4) * 4 + dy if axis == 0 else dx * 4 + (dy - k) % 4

    def target(axis, k):
        return (((ox + k) % 4) * 4 + oy, vir) if axis == 0 else (ox * 4 + (oy + k) % 4, vir)

    def send_sem(array):
        count[array] += 1
        return g_ss.at[array, count[array] - 1]

    def spread(array, axis, rel):
        source = shards[array] if rel == 0 else landing[array].at[rel - 1]
        copies = {}
        for k in (1, 3):
            there = step(rel, axis, k)
            copies[k] = push(
                source, landing[array].at[there - 1], send_sem(array), g_rs.at[array, there - 1, 0], target(axis, k)
            )
        return copies

    def forward(array, axis, rel, copies, flip):
        out = []
        for n, k in enumerate((1, 3)):
            copies[k].wait_recv()
            here = step(rel, axis, k)
            there = step(here, axis, k)
            which = (n + flip) % 2
            rows = pl.ds(*SUBS[which])
            out.append(push(
                landing[array].at[here - 1, rows], landing[array].at[there - 1, rows],
                send_sem(array), g_rs.at[array, there - 1, which], target(axis, k),
            ))
        return out

    first_axis, second_axis = (1, 0), (0, 1)
    first = [spread(array, first_axis[array], 0) for array in range(2)]
    second = [{0: spread(array, second_axis[array], 0)} for array in range(2)]
    turned = [[], []]

    tile_words()
    v_labels = [
        push(label_ref.at[k], v_label.at[VIR - k - 1], vl_ss.at[k - 1], vl_rs.at[VIR - k - 1], (occ, (vir + k) % VIR))
        for k in range(1, VIR)
    ]

    def v_pack(q, carry):
        for j in range(8):
            tile = t_ref[index_ref[q // 16, (q % 16) * 8 + j]]
            v_send[q // 4, q % 4, :, j * TILE : (j + 1) * TILE] = tile
        return carry

    lax.fori_loop(0, VIR * 4, v_pack, 0)

    def rows(h):
        return pl.ds(*CHUNKS[h])

    def v_push(h):
        return [
            push(v_send.at[k, :, rows(h)], v_got.at[VIR - k - 1, :, rows(h)], v_ss.at[h, k - 1], v_rs.at[h, VIR - k - 1],
                 (occ, (vir + k) % VIR))
            for k in range(1, VIR)
        ]

    v_copies = [v_push(h) for h in range(H)]

    middle = [forward(array, first_axis[array], 0, first[array], 0) for array in range(2)]
    for k in (1, 3):
        for array in range(2):
            rel = step(0, first_axis[array], k)
            second[array][rel] = spread(array, second_axis[array], rel)

    line = lax.broadcasted_iota(i32, (VCAP, 128), 0)
    lane = lax.broadcasted_iota(i32, (VCAP, 128), 1)
    places = [jnp.zeros((VCAP, 128), i32)] * 2
    infos = [jnp.zeros((VCAP, 128), i32)] * 2
    for k in range(VIR):
        if k == 0:
            label = label_ref[0]
        else:
            v_labels[VIR - k - 1].wait_recv()
            label = v_label[k - 1]
        for half in range(2):
            hit = (label >= 0) & ((label & 255) == lane + 128 * half)
            places[half] = places[half] + jnp.where(hit, line + k * VCAP, 0)
            infos[half] = infos[half] + jnp.where(hit, (label >> 8) + 1, 0)
    words[...] = jnp.zeros((16, 128), i32)
    for half in range(2):
        words[half : half + 1] = jnp.minimum(jnp.sum(places[half], axis=0, keepdims=True), VIR * VCAP - 1)
        info = jnp.sum(infos[half].astype(jnp.float32), axis=0, keepdims=True)
        column = jnp.transpose(jnp.broadcast_to(info, (128, 128))).astype(i32)
        o_label[half * 8 : half * 8 + 8] = column.reshape(8, 16, 128)
    to_scalar = pltpu.make_async_copy(words.at[0:8], o_index, w_sem.at[0])
    to_scalar.start()
    o_labels = [
        push(o_label.at[k], o_label_got.at[OCC - k - 1], ol_ss.at[k - 1], ol_rs.at[OCC - k - 1], ((occ + k) % OCC, vir))
        for k in range(1, OCC)
    ]
    to_scalar.wait()

    for array in range(2):
        for copy in middle[array]:
            copy.wait_recv()
        rel = step(step(0, first_axis[array], 1), first_axis[array], 1)
        second[array][rel] = spread(array, second_axis[array], rel)
    blocks[BLOCKS] = jnp.zeros((TILE, TILE), jnp.bfloat16)

    def gather_unpack(array):
        for copy in turned[array]:
            copy.wait_recv()

        def unpack_from(ref, base):
            left, right = ref[:, : 6 * TILE], ref[:, 6 * TILE :]
            strips = (left[:TILE], jnp.concatenate([left[TILE:], right[: 2 * TILE - FLAT]], axis=0), right[2 * TILE - FLAT :])
            for row in range(3):
                for c in range(6):
                    blocks[base + row * 6 + c] = strips[row][:, c * TILE : (c + 1) * TILE]

        unpack_from(shards[array], 0)

        def body(n, carry):
            unpack_from(landing[array].at[n], (n + 1) * 18)
            return carry

        lax.fori_loop(0, OCC - 1, body, 0)

    def cycle_words():
        line16 = lax.broadcasted_iota(i32, (16, 128), 0)
        totals = [jnp.zeros((16, 128), i32)] * 2
        o_line = lax.broadcasted_iota(i32, (PAIRS, OCC), 1)
        from_group = jnp.sum(jnp.where(map_ref[...] == occ, (o_line - occ) & 15, 0), axis=1, keepdims=True)
        from_group = jnp.broadcast_to(from_group, (PAIRS, 128))
        pair_of = [total(line16 == rows_ref[half, 0:1], from_group) for half in range(2)]
        live = [rows_ref[half, 0:1] >= 0 for half in range(2)]
        for k in range(OCC):
            if k == 0:
                label = o_label[0]
            else:
                o_labels[OCC - k - 1].wait_recv()
                label = o_label_got[k - 1]
            value = (line16 + k * 16) * 8 + ((label - 1) & 7) + 1
            for half in range(2):
                hit = (label > 0) & live[half] & (pair_of[half] == k) & (((label - 1) >> 3) == rows_ref[half, 1:2])
                totals[half] = totals[half] + jnp.where(hit, value, 0)
        for half in range(2):
            for j in range(2):
                found = jnp.sum(totals[half][j * 8 : j * 8 + 8], axis=0, keepdims=True)
                b = rows_ref[half, 2:3]
                third = (b * 171) >> 9
                base = ring_ahead(third) * 18 + b - 3 * third
                block = jnp.where(found > 0, base + 3 * ((found - 1) & 7), BLOCKS)
                tile = jnp.where(found > 0, (found - 1) >> 3, 0)
                words[8 + half * 4 + j : 9 + half * 4 + j] = jnp.clip(block, 0, BLOCKS)
                words[10 + half * 4 + j : 11 + half * 4 + j] = jnp.minimum(tile, 255)
        copy = pltpu.make_async_copy(words.at[8:16], c_index, w_sem.at[1])
        copy.start()
        copy.wait()

    def split(dst, strip, base):
        for j in range(8):
            dst[base + j] = strip[:, j * TILE : (j + 1) * TILE]

    def o_step(h):
        for copy in v_copies[h]:
            copy.wait_recv()
        tiles = small.at[:, pl.ds(0, CHUNKS[h][1])]
        for q in range(4):
            split(tiles, v_send[0, q, rows(h)], q * 8)

        def unpack(q, carry):
            split(tiles, v_got[q // 4, q % 4, rows(h)], (q + 4) * 8)
            return carry

        lax.fori_loop(0, (VIR - 1) * 4, unpack, 0)

        def pack(q, carry):
            for j in range(8):
                o_send[q // 2, q % 2, rows(h), j * TILE : (j + 1) * TILE] = tiles[o_index[q // 16, (q % 16) * 8 + j]]
            return carry

        lax.fori_loop(0, OCC * 2, pack, 0)
        return [
            push(o_send.at[k, :, rows(h)], o_got.at[OCC - k - 1, :, rows(h)], o_ss.at[h, k - 1],
                 o_rs.at[h, OCC - k - 1], ((occ + k) % OCC, vir))
            for k in range(1, OCC)
        ]

    def products(look, tiles, part, held, swap, dest):
        def octet(n, carry):
            side, i = n // 3, n % 3
            for j in range(8):
                row = ((dest * 2 + side) * 3 + i) * 8 + j
                total = None
                for half in range(2):
                    block = blocks[look(half, row)]
                    tile = tiles[look(2 + half, row)]
                    left, right = (tile, block) if swap else (block, tile)
                    term = jnp.dot(left, right, preferred_element_type=jnp.float32)
                    total = term if total is None else total + term
                part[side, dest, i, held, j * TILE : (j + 1) * TILE] = total.astype(jnp.bfloat16)
            return carry

        lax.fori_loop(0, 6, octet, 0)

    def core_push(n, k, part, dst, held):
        dest = (z + k) % 4
        return push(
            part.at[1 - core, dest, :, held], dst.at[dest, :, held],
            core_ss.at[n, k], core_rs.at[n, k], (occ, z * 2 + 1 - core),
        )

    def z_push(n, k, copy, part, dst, z_got, held):
        copy.wait_recv()
        dest = (z + k) % 4
        for i in range(3):
            total = part[core, dest, i, held].astype(jnp.float32) + dst[dest, i, held].astype(jnp.float32)
            dst[dest, i, held] = total.astype(jnp.bfloat16)
        if k == 0:
            return []
        return [push(
            dst.at[dest, :, held], z_got.at[4 - k - 1, :, held], z_ss.at[n, k - 1], z_rs.at[n, 4 - k - 1],
            (occ, dest * 2 + core),
        )]

    def all_rows(n, look, tiles, part, dst, z_got, held, swap):
        copies, before = [], None
        for k in (2, 1, 3, 0):
            products(look, tiles, part, held, swap, (z + k) % 4)
            copy = core_push(n, k, part, dst, held)
            if before is not None:
                copies = copies + z_push(n, before[0], before[1], part, dst, z_got, held)
            before = (k, copy)
        return copies, before

    def finish(copies, dst, z_got, out, held):
        for copy in copies:
            copy.wait_recv()
        for i in range(3):
            total = dst[z, i, held].astype(jnp.float32)
            for k in range(3):
                total = total + z_got[k, i, held].astype(jnp.float32)
            for j in range(8):
                out[i * 8 + j, held] = total[:, j * TILE : (j + 1) * TILE]

    whole = pl.ds(0, TILE)
    o_copies = []
    for n in range(4):
        for array in range(2):
            rel = list(second[array])[n]
            turned[array] = turned[array] + forward(array, second_axis[array], rel, second[array][rel], n % 2)
        if n == 1:
            o_copies.append(o_step(0))
    o_copies = o_copies + [o_step(h) for h in range(1, H)]
    gather_unpack(0)
    l_copies, rest = all_rows(
        H, lambda n, row: index_ref[2 + (row // 128) * 4 + n, row % 128], t_ref, l_part, l_core, l_z, whole, False
    )
    cycle_words()
    gather_unpack(1)
    l_copies = l_copies + z_push(H, *rest, l_part, l_core, l_z, whole)
    c_copies, rests = [], []
    for h in range(H):
        for copy in o_copies[h]:
            copy.wait_recv()
        tiles = small.at[:, pl.ds(0, CHUNKS[h][1])]
        for j in range(2):
            split(tiles, o_send[0, j, rows(h)], j * 8)

        def unpack(q, carry):
            split(tiles, o_got[q // 2, q % 2, rows(h)], (q + 2) * 8)
            return carry

        lax.fori_loop(0, (OCC - 1) * 2, unpack, 0)
        copies, rest = all_rows(
            h, lambda n, row: c_index[(row // 128) * 4 + n, row % 128], tiles, c_part, c_core, c_z, rows(h), True
        )
        c_copies.append(copies)
        rests.append(rest)
    finish(l_copies, l_core, l_z, ladder_ref, whole)
    for h in range(H):
        z_push(h, *rests[h], c_part, c_core, c_z, rows(h))
        finish(c_copies[h], c_core, c_z, cycle_ref, rows(h))
    for copy in sent:
        copy.wait_send()


def main_call(index, owners, rows, tiles, x, y):
    bf16 = jnp.bfloat16
    vmem = pl.BlockSpec(memory_space=pltpu.VMEM)
    dma = pltpu.SemaphoreType.DMA
    out = jax.ShapeDtypeStruct((24, TILE, TILE), jnp.float32)
    return pl.pallas_call(
        main_kernel,
        out_shape=(out, out),
        in_specs=[vmem] * 6,
        out_specs=(vmem, vmem),
        scratch_shapes=[
            pltpu.SMEM((16, 128), jnp.int32),
            pltpu.VMEM((VIR, VCAP, 128), jnp.int32),
            pltpu.VMEM((16, 128), jnp.int32),
            pltpu.VMEM((FLAT, 12 * TILE), bf16),
            pltpu.VMEM((FLAT, 12 * TILE), bf16),
            pltpu.VMEM((OCC - 1, FLAT, 12 * TILE), bf16),
            pltpu.VMEM((OCC - 1, FLAT, 12 * TILE), bf16),
            pltpu.VMEM((BLOCKS + 1, TILE, TILE), bf16),
            pltpu.VMEM((VIR, 4, TILE, WIDE), bf16),
            pltpu.VMEM((VIR - 1, 4, TILE, WIDE), bf16),
            pltpu.VMEM((OCC, 2, TILE, WIDE), bf16),
            pltpu.VMEM((OCC - 1, 2, TILE, WIDE), bf16),
            pltpu.VMEM((256, MOST, TILE), bf16),
            pltpu.VMEM((2, 4, 3, TILE, WIDE), bf16),
            pltpu.VMEM((4, 3, TILE, WIDE), bf16),
            pltpu.VMEM((3, 3, TILE, WIDE), bf16),
            pltpu.VMEM((2, 4, 3, TILE, WIDE), bf16),
            pltpu.VMEM((4, 3, TILE, WIDE), bf16),
            pltpu.VMEM((3, 3, TILE, WIDE), bf16),
            pltpu.VMEM((VIR - 1, VCAP, 128), jnp.int32),
            pltpu.VMEM((OCC, 16, 128), jnp.int32),
            pltpu.VMEM((OCC - 1, 16, 128), jnp.int32),
            pltpu.VMEM((16, 128), jnp.int32),
            pltpu.SMEM((8, 128), jnp.int32),
            pltpu.SMEM((8, 128), jnp.int32),
            dma((2, 20)), dma((2, OCC - 1, 2)),
            dma((H, VIR - 1)), dma((H, VIR - 1)),
            dma((H, OCC - 1)), dma((H, OCC - 1)),
            dma((H + 1, 4)), dma((H + 1, 4)),
            dma((H + 1, 3)), dma((H + 1, 3)),
            dma((VIR - 1,)), dma((VIR - 1,)), dma((OCC - 1,)), dma((OCC - 1,)), dma((3,)),
        ],
        compiler_params=pltpu.CompilerParams(
            collective_id=1, has_side_effects=True, vmem_limit_bytes=63_000_000
        ),
        cost_estimate=pl.CostEstimate(flops=8 * ROWS * TILE**3, bytes_accessed=14_000_000, transcendentals=0),
        name="contract",
    )(index, owners, rows, tiles, x, y)


def on_device(t_tiles, t_index, cycle_map, ladder_slots, cycle_slots, x_ints, y_ints):
    slots = jnp.concatenate([cycle_slots, ladder_slots], axis=1).T
    rows = jnp.pad(slots, ((0, 2), (0, 256 - ROWS)), constant_values=-1).reshape(8, 2, 128).transpose(1, 0, 2)
    owners = cycle_map.reshape(OCC, PAIRS).T
    ladder, cycle = main_call(t_index, owners, rows, t_tiles.reshape(128, TILE, TILE), x_ints, y_ints.T)
    return ladder.reshape(24, AREA), cycle.reshape(24, AREA)


def solution(mesh):
    return jax.shard_map(
        on_device,
        mesh=mesh,
        in_specs=(
            P(("occ", "vir"), None),
            P(("occ", "vir"), None),
            P(),
            P("occ", None),
            P("occ", None),
            P("occ", "vir"),
            P("vir", "occ"),
        ),
        out_specs=(P(("occ", "vir"), None), P(("occ", "vir"), None)),
        check_vma=False,
    )
```

```python
import functools

import jax
import jax.numpy as jnp
from jax import lax
from jax.experimental import pallas as pl
from jax.experimental.pallas import tpu as pltpu
from jax.sharding import PartitionSpec as P

TILE = 96
NV = 48
AREA = TILE * TILE
OCC = 16
VIR = 8
VT = 6
PAIRS = 16
VCAP = 32
BLOCKS = 288
ROWS = 192
WIDE = 8 * TILE
CHUNKS = ((0, 32), (32, 32), (64, 32))
H = len(CHUNKS)
MOST = max(n for _, n in CHUNKS)
FLAT = 144
SUBS = ((0, 80), (80, 64))
MESH = pl.DeviceIdType.MESH


def main_kernel(
    list_ref, map_ref, rows_ref, t_ref, x_ref, y_ref, ladder_ref, cycle_ref,
    index_ref, label_ref, first_words,
    x_flat, y_flat, x_got, y_got, blocks, v_send, v_got, o_send, o_got, small,
    l_part, l_core, l_z, c_part, c_core, c_z,
    v_label, o_label, o_label_got, words, o_index, c_index,
    g_ss, g_rs, v_ss, v_rs, o_ss, o_rs, core_ss, core_rs, z_ss, z_rs,
    vl_ss, vl_rs, ol_ss, ol_rs, w_sem,
):
    occ, vir = lax.axis_index("occ"), lax.axis_index("vir")
    ox, oy = occ // 4, occ % 4
    z, core = vir // 2, vir % 2
    i32 = jnp.int32
    barrier = pltpu.get_barrier_semaphore()
    for k in range(1, VIR):
        pl.semaphore_signal(barrier, inc=1, device_id=(occ, (vir + k) % VIR), device_id_type=MESH)
    for k in range(1, OCC):
        pl.semaphore_signal(barrier, inc=1, device_id=((occ + k) % OCC, vir), device_id_type=MESH)

    for part in range(2):
        x_flat[:, part * 6 * TILE : (part + 1) * 6 * TILE] = x_ref[part * FLAT : (part + 1) * FLAT]
    for d in range(6):
        first_row, lane = (d // 2) * TILE, (d % 2) * 3 * TILE
        strip = jnp.transpose(y_ref[:, d * TILE : (d + 1) * TILE])
        for start in range(0, TILE, 48):
            row = first_row + start
            shift = (row // FLAT) * 6 * TILE + lane
            y_flat[row % FLAT : row % FLAT + 48, shift : shift + 3 * TILE] = strip[start : start + 48]
    pl.semaphore_wait(barrier, VIR + OCC - 2)
    sent = []

    def push(src, dst, ssem, rsem, device):
        copy = pltpu.make_async_remote_copy(src, dst, ssem, rsem, device_id=device, device_id_type=MESH)
        copy.start()
        sent.append(copy)
        return copy

    def column(row):
        return jnp.transpose(jnp.broadcast_to(row.astype(jnp.float32), (128, 128))).astype(i32)

    def total(mask, value=1):
        return jnp.sum(jnp.where(mask, value, 0), axis=0, keepdims=True)

    def tile_words():
        lane = lax.broadcasted_iota(i32, (128, 128), 1)
        at = [jnp.broadcast_to(list_ref[:, n : n + 1], (128, 128)) for n in range(3)]
        local, first, second = at[0] - occ * PAIRS, at[1], at[2]
        group = (second * 43) >> 8
        k_local, k_first, k_second = (jnp.transpose(v.astype(jnp.float32)).astype(i32) for v in (local, first, second))
        k_group = (k_second * 43) >> 8
        same = (local == k_local) & (first == k_first)
        smaller = same & (second < k_first)
        here = same & (group == vir)
        together = group == k_group
        rank_all, which, own_count = total(smaller), total(smaller & here), total(here)
        rank_second = total(same & together & (second < k_second))
        start = total(together & (local < k_local))
        k_local, k_first, k_second, k_group = (v[0:1] for v in (k_local, k_first, k_second, k_group))

        position = ((k_group - vir) & 7) * VCAP + start + rank_second * own_count + which
        one = lax.broadcasted_iota(i32, (PAIRS, OCC), 1) == occ
        ahead = (jnp.sum(jnp.where(one, map_ref[...], 0), axis=1, keepdims=True) - occ) & 15
        to_group = total(lax.broadcasted_iota(i32, (PAIRS, 128), 0) == k_local, jnp.broadcast_to(ahead, (PAIRS, 128)))
        label = to_group * 16 + rank_second * 8 + rank_all + 256 * (k_first * 8 + k_second - 6 * k_group)
        places = column(position)
        values = column(label * 128 + lane[0:1] + 1)
        first_words[...] = jnp.zeros((16, 128), i32)
        for half in range(2):
            found = total(places == lane + 128 * half, values)
            first_words[half : half + 1] = jnp.where(found > 0, (found - 1) & 127, 0)
            went = column(jnp.where(found > 0, (found - 1) >> 7, -1))
            label_ref[half * 4 : half * 4 + 4] = went.reshape(4, VCAP, 128)

        keys = column((k_local * 2 + which) * NV + k_second)
        values = column(lane[0:1] * 8 + k_first - vir * VT + 1)
        for half in range(2):
            s, a, b = (rows_ref[half, n : n + 1] for n in (3, 4, 5))
            third = (a * 171) >> 9
            base = (ring_ahead(third) * 3 + a - 3 * third) * VT
            for j in range(2):
                found = total(keys == (s * 2 + j) * NV + b, values)
                block = jnp.where(found > 0, base + ((found - 1) & 7), BLOCKS)
                tile = jnp.where(found > 0, (found - 1) >> 3, 0)
                first_words[2 + half * 4 + j : 3 + half * 4 + j] = jnp.clip(block, 0, BLOCKS)
                first_words[4 + half * 4 + j : 5 + half * 4 + j] = jnp.clip(tile, 0, 127)
        copy = pltpu.make_async_copy(first_words, index_ref, w_sem.at[2])
        copy.start()
        copy.wait()

    def ring_ahead(group):
        return (((group >> 2) - ox) & 3) * 4 + (((group & 3) - oy) & 3)

    shards = (x_flat, y_flat)
    landing = (x_got, y_got)
    count = [0, 0]

    def step(rel, axis, k):
        dx, dy = rel // 4, rel % 4
        return ((dx - k) % 4) * 4 + dy if axis == 0 else dx * 4 + (dy - k) % 4

    def target(axis, k):
        return (((ox + k) % 4) * 4 + oy, vir) if axis == 0 else (ox * 4 + (oy + k) % 4, vir)

    def send_sem(array):
        count[array] += 1
        return g_ss.at[array, count[array] - 1]

    def spread(array, axis, rel):
        source = shards[array] if rel == 0 else landing[array].at[rel - 1]
        copies = {}
        for k in (1, 3):
            there = step(rel, axis, k)
            copies[k] = push(
                source, landing[array].at[there - 1], send_sem(array), g_rs.at[array, there - 1, 0], target(axis, k)
            )
        return copies

    def forward(array, axis, rel, copies, flip):
        out = []
        for n, k in enumerate((1, 3)):
            copies[k].wait_recv()
            here = step(rel, axis, k)
            there = step(here, axis, k)
            which = (n + flip) % 2
            rows = pl.ds(*SUBS[which])
            out.append(push(
                landing[array].at[here - 1, rows], landing[array].at[there - 1, rows],
                send_sem(array), g_rs.at[array, there - 1, which], target(axis, k),
            ))
        return out

    first_axis, second_axis = (1, 0), (0, 1)
    first = [spread(array, first_axis[array], 0) for array in range(2)]
    second = [{0: spread(array, second_axis[array], 0)} for array in range(2)]
    turned = [[], []]

    tile_words()
    v_labels = [
        push(label_ref.at[k], v_label.at[VIR - k - 1], vl_ss.at[k - 1], vl_rs.at[VIR - k - 1], (occ, (vir + k) % VIR))
        for k in range(1, VIR)
    ]

    def v_pack(q, carry):
        for j in range(8):
            tile = t_ref[index_ref[q // 16, (q % 16) * 8 + j]]
            v_send[q // 4, q % 4, :, j * TILE : (j + 1) * TILE] = tile
        return carry

    lax.fori_loop(0, VIR * 4, v_pack, 0)

    def rows(h):
        return pl.ds(*CHUNKS[h])

    def v_push(h):
        return [
            push(v_send.at[k, :, rows(h)], v_got.at[VIR - k - 1, :, rows(h)], v_ss.at[h, k - 1], v_rs.at[h, VIR - k - 1],
                 (occ, (vir + k) % VIR))
            for k in range(1, VIR)
        ]

    v_copies = [v_push(h) for h in range(H)]

    middle = [forward(array, first_axis[array], 0, first[array], 0) for array in range(2)]
    for k in (1, 3):
        for array in range(2):
            rel = step(0, first_axis[array], k)
            second[array][rel] = spread(array, second_axis[array], rel)

    line = lax.broadcasted_iota(i32, (VCAP, 128), 0)
    lane = lax.broadcasted_iota(i32, (VCAP, 128), 1)
    places = [jnp.zeros((VCAP, 128), i32)] * 2
    infos = [jnp.zeros((VCAP, 128), i32)] * 2
    for k in range(VIR):
        if k == 0:
            label = label_ref[0]
        else:
            v_labels[VIR - k - 1].wait_recv()
            label = v_label[k - 1]
        for half in range(2):
            hit = (label >= 0) & ((label & 255) == lane + 128 * half)
            places[half] = places[half] + jnp.where(hit, line + k * VCAP, 0)
            infos[half] = infos[half] + jnp.where(hit, (label >> 8) + 1, 0)
    words[...] = jnp.zeros((16, 128), i32)
    for half in range(2):
        words[half : half + 1] = jnp.minimum(jnp.sum(places[half], axis=0, keepdims=True), VIR * VCAP - 1)
        info = jnp.sum(infos[half].astype(jnp.float32), axis=0, keepdims=True)
        column = jnp.transpose(jnp.broadcast_to(info, (128, 128))).astype(i32)
        o_label[half * 8 : half * 8 + 8] = column.reshape(8, 16, 128)
    to_scalar = pltpu.make_async_copy(words.at[0:8], o_index, w_sem.at[0])
    to_scalar.start()
    o_labels = [
        push(o_label.at[k], o_label_got.at[OCC - k - 1], ol_ss.at[k - 1], ol_rs.at[OCC - k - 1], ((occ + k) % OCC, vir))
        for k in range(1, OCC)
    ]
    to_scalar.wait()

    for array in range(2):
        for copy in middle[array]:
            copy.wait_recv()
        rel = step(step(0, first_axis[array], 1), first_axis[array], 1)
        second[array][rel] = spread(array, second_axis[array], rel)
    blocks[BLOCKS] = jnp.zeros((TILE, TILE), jnp.bfloat16)

    def gather_unpack(array):
        for copy in turned[array]:
            copy.wait_recv()

        def unpack_from(ref, base):
            left, right = ref[:, : 6 * TILE], ref[:, 6 * TILE :]
            strips = (left[:TILE], jnp.concatenate([left[TILE:], right[: 2 * TILE - FLAT]], axis=0), right[2 * TILE - FLAT :])
            for row in range(3):
                for c in range(6):
                    blocks[base + row * 6 + c] = strips[row][:, c * TILE : (c + 1) * TILE]

        unpack_from(shards[array], 0)

        def body(n, carry):
            unpack_from(landing[array].at[n], (n + 1) * 18)
            return carry

        lax.fori_loop(0, OCC - 1, body, 0)

    def cycle_words():
        line16 = lax.broadcasted_iota(i32, (16, 128), 0)
        totals = [jnp.zeros((16, 128), i32)] * 2
        o_line = lax.broadcasted_iota(i32, (PAIRS, OCC), 1)
        from_group = jnp.sum(jnp.where(map_ref[...] == occ, (o_line - occ) & 15, 0), axis=1, keepdims=True)
        from_group = jnp.broadcast_to(from_group, (PAIRS, 128))
        pair_of = [total(line16 == rows_ref[half, 0:1], from_group) for half in range(2)]
        live = [rows_ref[half, 0:1] >= 0 for half in range(2)]
        for k in range(OCC):
            if k == 0:
                label = o_label[0]
            else:
                o_labels[OCC - k - 1].wait_recv()
                label = o_label_got[k - 1]
            value = (line16 + k * 16) * 8 + ((label - 1) & 7) + 1
            for half in range(2):
                hit = (label > 0) & live[half] & (pair_of[half] == k) & (((label - 1) >> 3) == rows_ref[half, 1:2])
                totals[half] = totals[half] + jnp.where(hit, value, 0)
        for half in range(2):
            for j in range(2):
                found = jnp.sum(totals[half][j * 8 : j * 8 + 8], axis=0, keepdims=True)
                b = rows_ref[half, 2:3]
                third = (b * 171) >> 9
                base = ring_ahead(third) * 18 + b - 3 * third
                block = jnp.where(found > 0, base + 3 * ((found - 1) & 7), BLOCKS)
                tile = jnp.where(found > 0, (found - 1) >> 3, 0)
                words[8 + half * 4 + j : 9 + half * 4 + j] = jnp.clip(block, 0, BLOCKS)
                words[10 + half * 4 + j : 11 + half * 4 + j] = jnp.minimum(tile, 255)
        copy = pltpu.make_async_copy(words.at[8:16], c_index, w_sem.at[1])
        copy.start()
        copy.wait()

    def split(dst, strip, base):
        for j in range(8):
            dst[base + j] = strip[:, j * TILE : (j + 1) * TILE]

    def o_step(h):
        for copy in v_copies[h]:
            copy.wait_recv()
        tiles = small.at[:, pl.ds(0, CHUNKS[h][1])]
        for q in range(4):
            split(tiles, v_send[0, q, rows(h)], q * 8)

        def unpack(q, carry):
            split(tiles, v_got[q // 4, q % 4, rows(h)], (q + 4) * 8)
            return carry

        lax.fori_loop(0, (VIR - 1) * 4, unpack, 0)

        def pack(q, carry):
            for j in range(8):
                o_send[q // 2, q % 2, rows(h), j * TILE : (j + 1) * TILE] = tiles[o_index[q // 16, (q % 16) * 8 + j]]
            return carry

        lax.fori_loop(0, OCC * 2, pack, 0)
        return [
            push(o_send.at[k, :, rows(h)], o_got.at[OCC - k - 1, :, rows(h)], o_ss.at[h, k - 1],
                 o_rs.at[h, OCC - k - 1], ((occ + k) % OCC, vir))
            for k in (10, 6, 14, 9, 11, 2, 8, 5, 7, 13, 15, 1, 3, 4, 12)
        ]

    def products(look, tiles, part, held, swap, dest):
        def octet(n, carry):
            side, i = n // 3, n % 3
            for j in range(8):
                row = ((dest * 2 + side) * 3 + i) * 8 + j
                total = None
                for half in range(2):
                    block = blocks[look(half, row)]
                    tile = tiles[look(2 + half, row)]
                    left, right = (tile, block) if swap else (block, tile)
                    term = jnp.dot(left, right, preferred_element_type=jnp.float32)
                    total = term if total is None else total + term
                part[side, dest, i, held, j * TILE : (j + 1) * TILE] = total.astype(jnp.bfloat16)
            return carry

        lax.fori_loop(0, 6, octet, 0)

    def core_push(n, k, part, dst, held):
        dest = (z + k) % 4
        return push(
            part.at[1 - core, dest, :, held], dst.at[dest, :, held],
            core_ss.at[n, k], core_rs.at[n, k], (occ, z * 2 + 1 - core),
        )

    def z_push(n, k, copy, part, dst, z_got, held):
        copy.wait_recv()
        dest = (z + k) % 4
        for i in range(3):
            total = part[core, dest, i, held].astype(jnp.float32) + dst[dest, i, held].astype(jnp.float32)
            dst[dest, i, held] = total.astype(jnp.bfloat16)
        if k == 0:
            return []
        return [push(
            dst.at[dest, :, held], z_got.at[4 - k - 1, :, held], z_ss.at[n, k - 1], z_rs.at[n, 4 - k - 1],
            (occ, dest * 2 + core),
        )]

    def all_rows(n, look, tiles, part, dst, z_got, held, swap):
        copies, before = [], None
        for k in (2, 1, 3, 0):
            products(look, tiles, part, held, swap, (z + k) % 4)
            copy = core_push(n, k, part, dst, held)
            if before is not None:
                copies = copies + z_push(n, before[0], before[1], part, dst, z_got, held)
            before = (k, copy)
        return copies, before

    def finish(copies, dst, z_got, out, held):
        for copy in copies:
            copy.wait_recv()
        for i in range(3):
            total = dst[z, i, held].astype(jnp.float32)
            for k in range(3):
                total = total + z_got[k, i, held].astype(jnp.float32)
            for j in range(8):
                out[i * 8 + j, held] = total[:, j * TILE : (j + 1) * TILE]

    whole = pl.ds(0, TILE)
    o_copies = []
    for n in range(4):
        for array in range(2):
            rel = list(second[array])[n]
            turned[array] = turned[array] + forward(array, second_axis[array], rel, second[array][rel], n % 2)
        if n == 1:
            o_copies.append(o_step(0))
    o_copies = o_copies + [o_step(h) for h in range(1, H)]
    gather_unpack(0)
    l_copies, rest = all_rows(
        H, lambda n, row: index_ref[2 + (row // 128) * 4 + n, row % 128], t_ref, l_part, l_core, l_z, whole, False
    )
    cycle_words()
    gather_unpack(1)
    l_copies = l_copies + z_push(H, *rest, l_part, l_core, l_z, whole)
    c_copies, rests = [], []
    for h in range(H):
        for copy in o_copies[h]:
            copy.wait_recv()
        tiles = small.at[:, pl.ds(0, CHUNKS[h][1])]
        for j in range(2):
            split(tiles, o_send[0, j, rows(h)], j * 8)

        def unpack(q, carry):
            split(tiles, o_got[q // 2, q % 2, rows(h)], (q + 2) * 8)
            return carry

        lax.fori_loop(0, (OCC - 1) * 2, unpack, 0)
        copies, rest = all_rows(
            h, lambda n, row: c_index[(row // 128) * 4 + n, row % 128], tiles, c_part, c_core, c_z, rows(h), True
        )
        c_copies.append(copies)
        rests.append(rest)
    finish(l_copies, l_core, l_z, ladder_ref, whole)
    for h in range(H):
        z_push(h, *rests[h], c_part, c_core, c_z, rows(h))
        finish(c_copies[h], c_core, c_z, cycle_ref, rows(h))
    for copy in sent:
        copy.wait_send()


def main_call(index, owners, rows, tiles, x, y):
    bf16 = jnp.bfloat16
    vmem = pl.BlockSpec(memory_space=pltpu.VMEM)
    dma = pltpu.SemaphoreType.DMA
    out = jax.ShapeDtypeStruct((24, TILE, TILE), jnp.float32)
    return pl.pallas_call(
        main_kernel,
        out_shape=(out, out),
        in_specs=[vmem] * 6,
        out_specs=(vmem, vmem),
        scratch_shapes=[
            pltpu.SMEM((16, 128), jnp.int32),
            pltpu.VMEM((VIR, VCAP, 128), jnp.int32),
            pltpu.VMEM((16, 128), jnp.int32),
            pltpu.VMEM((FLAT, 12 * TILE), bf16),
            pltpu.VMEM((FLAT, 12 * TILE), bf16),
            pltpu.VMEM((OCC - 1, FLAT, 12 * TILE), bf16),
            pltpu.VMEM((OCC - 1, FLAT, 12 * TILE), bf16),
            pltpu.VMEM((BLOCKS + 1, TILE, TILE), bf16),
            pltpu.VMEM((VIR, 4, TILE, WIDE), bf16),
            pltpu.VMEM((VIR - 1, 4, TILE, WIDE), bf16),
            pltpu.VMEM((OCC, 2, TILE, WIDE), bf16),
            pltpu.VMEM((OCC - 1, 2, TILE, WIDE), bf16),
            pltpu.VMEM((256, MOST, TILE), bf16),
            pltpu.VMEM((2, 4, 3, TILE, WIDE), bf16),
            pltpu.VMEM((4, 3, TILE, WIDE), bf16),
            pltpu.VMEM((3, 3, TILE, WIDE), bf16),
            pltpu.VMEM((2, 4, 3, TILE, WIDE), bf16),
            pltpu.VMEM((4, 3, TILE, WIDE), bf16),
            pltpu.VMEM((3, 3, TILE, WIDE), bf16),
            pltpu.VMEM((VIR - 1, VCAP, 128), jnp.int32),
            pltpu.VMEM((OCC, 16, 128), jnp.int32),
            pltpu.VMEM((OCC - 1, 16, 128), jnp.int32),
            pltpu.VMEM((16, 128), jnp.int32),
            pltpu.SMEM((8, 128), jnp.int32),
            pltpu.SMEM((8, 128), jnp.int32),
            dma((2, 20)), dma((2, OCC - 1, 2)),
            dma((H, VIR - 1)), dma((H, VIR - 1)),
            dma((H, OCC - 1)), dma((H, OCC - 1)),
            dma((H + 1, 4)), dma((H + 1, 4)),
            dma((H + 1, 3)), dma((H + 1, 3)),
            dma((VIR - 1,)), dma((VIR - 1,)), dma((OCC - 1,)), dma((OCC - 1,)), dma((3,)),
        ],
        compiler_params=pltpu.CompilerParams(
            collective_id=1, has_side_effects=True, vmem_limit_bytes=63_000_000
        ),
        cost_estimate=pl.CostEstimate(flops=8 * ROWS * TILE**3, bytes_accessed=14_000_000, transcendentals=0),
        name="contract",
    )(index, owners, rows, tiles, x, y)


def on_device(t_tiles, t_index, cycle_map, ladder_slots, cycle_slots, x_ints, y_ints):
    slots = jnp.concatenate([cycle_slots, ladder_slots], axis=1).T
    rows = jnp.pad(slots, ((0, 2), (0, 256 - ROWS)), constant_values=-1).reshape(8, 2, 128).transpose(1, 0, 2)
    owners = cycle_map.reshape(OCC, PAIRS).T
    ladder, cycle = main_call(t_index, owners, rows, t_tiles.reshape(128, TILE, TILE), x_ints, y_ints.T)
    return ladder.reshape(24, AREA), cycle.reshape(24, AREA)


def solution(mesh):
    return jax.shard_map(
        on_device,
        mesh=mesh,
        in_specs=(
            P(("occ", "vir"), None),
            P(("occ", "vir"), None),
            P(),
            P("occ", None),
            P("occ", None),
            P("occ", "vir"),
            P("vir", "occ"),
        ),
        out_specs=(P(("occ", "vir"), None), P(("occ", "vir"), None)),
        check_vma=False,
    )
```
